32 devices in a mesh: ctx: 4 (over z), fsdp: 8 (over y, x, core).
Axes of the slice: x: 2, y: 2, z: 4, core: 2. Of those that a mesh axis runs over, the one named last changes fastest.
Arguments:
- hidden: bfloat16 [16, 1024, 2048], P('fsdp', 'ctx'), may hold values from -6 to 6
- cotangent: bfloat16 [16, 1024, 2048], P('fsdp', 'ctx'), may hold values from -6 to 6
- lengths: int32 [16], P('fsdp'), may hold values from 256 to 1024, as said below
- positions: int32 [16, 1024], P('fsdp', 'ctx'), may hold values from 0 to 3069, as said below
- query_key_value_master: float32 [2048, 4096], P(('ctx', 'fsdp')), may hold values from -0.125 to 0.125
- query_key_value_first: float32 [2048, 4096], P(('ctx', 'fsdp')), may hold values from -768 to 768
- query_key_value_second: float32 [2048, 4096], P(('ctx', 'fsdp')), may hold values from 16384 to 65536
- out_master: float32 [2048, 2048], P(('ctx', 'fsdp')), may hold values from -1.5 to 1.5
- out_first: float32 [2048, 2048], P(('ctx', 'fsdp')), may hold values from -64 to 64
- out_second: float32 [2048, 2048], P(('ctx', 'fsdp')), may hold values from 128 to 512
- gateup_master: float32 [2048, 16384], P(('ctx', 'fsdp')), may hold values from -0.125 to 0.125
- gateup_first: float32 [2048, 16384], P(('ctx', 'fsdp')), may hold values from -192 to 192
- gateup_second: float32 [2048, 16384], P(('ctx', 'fsdp')), may hold values from 1024 to 4096
- down_master: float32 [8192, 2048], P(('ctx', 'fsdp')), may hold values from -0.0625 to 0.0625
- down_first: float32 [8192, 2048], P(('ctx', 'fsdp')), may hold values from -384 to 384
- down_second: float32 [8192, 2048], P(('ctx', 'fsdp')), may hold values from 4096 to 16384
- gains_master: float32 [2, 2048], P(None, ('ctx', 'fsdp')), may hold values from 0.5 to 1.5
- gains_first: float32 [2, 2048], P(None, ('ctx', 'fsdp')), may hold values from -768 to 768
- gains_second: float32 [2, 2048], P(None, ('ctx', 'fsdp')), may hold values from 16384 to 65536
Outputs:
- output: bfloat16 [16, 1024, 2048], P('fsdp', 'ctx')
- input_grad: bfloat16 [16, 1024, 2048], P('fsdp', 'ctx')
- qkv_new: float32 [2048, 4096], P(('ctx', 'fsdp'))
- qkv_first_new: float32 [2048, 4096], P(('ctx', 'fsdp'))
- qkv_second_new: float32 [2048, 4096], P(('ctx', 'fsdp'))
- qkv_copy: bfloat16 [2048, 4096], P(('ctx', 'fsdp'))
- out_new: float32 [2048, 2048], P(('ctx', 'fsdp'))
- out_first_new: float32 [2048, 2048], P(('ctx', 'fsdp'))
- out_second_new: float32 [2048, 2048], P(('ctx', 'fsdp'))
- out_copy: bfloat16 [2048, 2048], P(('ctx', 'fsdp'))
- gateup_new: float32 [2048, 16384], P(('ctx', 'fsdp'))
- gateup_first_new: float32 [2048, 16384], P(('ctx', 'fsdp'))
- gateup_second_new: float32 [2048, 16384], P(('ctx', 'fsdp'))
- gateup_copy: bfloat16 [2048, 16384], P(('ctx', 'fsdp'))
- down_new: float32 [8192, 2048], P(('ctx', 'fsdp'))
- down_first_new: float32 [8192, 2048], P(('ctx', 'fsdp'))
- down_second_new: float32 [8192, 2048], P(('ctx', 'fsdp'))
- down_copy: bfloat16 [8192, 2048], P(('ctx', 'fsdp'))
- gains_new: float32 [2, 2048], P(None, ('ctx', 'fsdp'))
- gains_first_new: float32 [2, 2048], P(None, ('ctx', 'fsdp'))
- gains_second_new: float32 [2, 2048], P(None, ('ctx', 'fsdp'))
- gains_copy: bfloat16 [2, 2048], P(None, ('ctx', 'fsdp'))
The draws below stay inside these ranges and needn't reach their ends.
Inputs may be any that keep to these rules, and one draw needn't show every extreme that they name: `lengths`: each group of 2 consecutive sequences holds one sequence of exactly 1024 valid slots. positions[s, 0] is at most 2046, along each sequence a position exceeds the one before it by 1 or 2, and one sequence ends exactly at the largest position.
All inputs are finite; a program needn't handle non-finite values.
Results may differ from the reference program's by a relative error of at most 0.02.
Values may be sent and summed in bfloat16 or wider, within the bound.
No kernel may reach another device: no remote copies, remote signals or barrier semaphores. Data moves between devices by JAX's collectives and lax.ppermute only.
A program may use at most 576 MiB of HBM per device.

```python
import math
import jax
import jax.numpy as jnp
from jax import lax

MODEL_DIM = 2048
QUERY_HEADS = 8
KEY_VALUE_HEADS = 4
HEAD_DIM = 256
FF = 8192
SEQ_DEV = 2
STEP = 10
SEQUENCE_LENGTH = 1024
SEQUENCE_TOTAL = 16


def draw_lengths(key, part):
    key = jax.random.fold_in(key, 11)
    key_len, key_pick = jax.random.split(key)
    drawn = jax.random.randint(key_len, (SEQUENCE_TOTAL // SEQ_DEV, SEQ_DEV), SEQUENCE_LENGTH // 4, SEQUENCE_LENGTH + 1)
    picked = jax.random.randint(key_pick, (SEQUENCE_TOTAL // SEQ_DEV, 1), 0, SEQ_DEV)
    member = jnp.arange(SEQ_DEV, dtype=jnp.int32)[None, :]
    full_len = jnp.full_like(drawn, SEQUENCE_LENGTH)
    return jnp.where(member == picked, full_len, drawn).reshape(SEQUENCE_TOTAL).astype(jnp.int32)


def draw_positions(key, part):
    key = jax.random.fold_in(key, 17)
    key_off, key_gap, key_pick = jax.random.split(key, 3)
    offsets = jax.random.randint(key_off, (SEQUENCE_TOTAL, 1), 0, SEQUENCE_LENGTH)
    gaps = jax.random.randint(key_gap, (SEQUENCE_TOTAL, SEQUENCE_LENGTH), 1, 3)
    first_col = jnp.arange(SEQUENCE_LENGTH, dtype=jnp.int32)[None, :] == 0
    gaps = jnp.where(first_col, 0, gaps).astype(jnp.int32)
    steps_total = jnp.sum(gaps, axis=1, keepdims=True).astype(jnp.int32)
    picked = jax.random.randint(key_pick, (), 0, SEQUENCE_TOTAL)
    row_ids = jnp.arange(SEQUENCE_TOTAL, dtype=jnp.int32)[:, None]
    top_start = (3 * SEQUENCE_LENGTH - 3 - steps_total).astype(jnp.int32)
    offsets = jnp.where(row_ids == picked, top_start, offsets).astype(jnp.int32)
    return (offsets + jnp.cumsum(gaps, axis=1)).astype(jnp.int32)


def steps_of(own_key, dims, shards, least, largest):
    factor_of = 1.0
    for axis_at, parts in shards:
        steps = jax.random.uniform(jax.random.fold_in(jax.random.fold_in(own_key, 6), axis_at), (parts,), jnp.float32, least / len(shards), largest / len(shards))
        factor_of = factor_of * jnp.repeat(jnp.exp(steps), dims[axis_at] // parts).reshape((-1,) + (1,) * (len(dims) - 1 - axis_at))
    return factor_of


def scatter_about(rng, shape, width, limit, shards=(), kind=jnp.bfloat16):
    array = width * jax.random.normal(rng, shape, jnp.float32)
    if shards:
        array = array * steps_of(rng, shape, shards, -0.22, 0.18)
    return jnp.clip(array, -limit, limit).astype(kind)


def setup_inputs(seed: int = 0) -> dict:
    seeds = jax.random.split(jax.random.key(seed), 20)
    return {
        "hidden": scatter_about(seeds[0], (SEQUENCE_TOTAL, SEQUENCE_LENGTH, MODEL_DIM), 1.0, 6.0, ((0, 8), (1, 4))),
        "cotangent": scatter_about(seeds[1], (SEQUENCE_TOTAL, SEQUENCE_LENGTH, MODEL_DIM), 1.0, 6.0, ((0, 8), (1, 4))),
        "lengths": draw_lengths(jax.random.fold_in(seeds[19], 71), 0),
        "positions": draw_positions(jax.random.fold_in(seeds[19], 71), 0),
        "query_key_value_master": scatter_about(seeds[4], (MODEL_DIM, MODEL_DIM + 2 * KEY_VALUE_HEADS * HEAD_DIM), MODEL_DIM ** -0.5, 0.125, ((0, 32),), jnp.float32),
        "query_key_value_first": scatter_about(seeds[5], (MODEL_DIM, MODEL_DIM + 2 * KEY_VALUE_HEADS * HEAD_DIM), ((SEQUENCE_TOTAL * SEQUENCE_LENGTH) ** 0.5), 768.0, ((0, 32),), jnp.float32),
        "query_key_value_second": jnp.clip(jnp.exp(math.log(65536.0) - 1.3862944 * jax.random.uniform(seeds[6], (MODEL_DIM, MODEL_DIM + 2 * KEY_VALUE_HEADS * HEAD_DIM), jnp.float32) ** steps_of(seeds[6], (MODEL_DIM, MODEL_DIM + 2 * KEY_VALUE_HEADS * HEAD_DIM), ((0, 32),), -0.2, 0.2)), 16384.0, 65536.0),
        "out_master": scatter_about(seeds[7], (MODEL_DIM, MODEL_DIM), (max(8 * MODEL_DIM // SEQUENCE_LENGTH, 1)) ** -0.5, 1.5, ((0, 32),), jnp.float32),
        "out_first": scatter_about(seeds[8], (MODEL_DIM, MODEL_DIM), ((8 * SEQUENCE_TOTAL) ** 0.5), 64.0, ((0, 32),), jnp.float32),
        "out_second": jnp.clip(jnp.exp(math.log(512.0) - 1.3862944 * jax.random.uniform(seeds[9], (MODEL_DIM, MODEL_DIM), jnp.float32) ** steps_of(seeds[9], (MODEL_DIM, MODEL_DIM), ((0, 32),), -0.2, 0.2)), 128.0, 512.0),
        "gateup_master": scatter_about(seeds[10], (MODEL_DIM, 2 * FF), MODEL_DIM ** -0.5, 0.125, ((0, 32),), jnp.float32),
        "gateup_first": scatter_about(seeds[11], (MODEL_DIM, 2 * FF), (0.25 * (SEQUENCE_TOTAL * SEQUENCE_LENGTH) ** 0.5), 192.0, ((0, 32),), jnp.float32),
        "gateup_second": jnp.clip(jnp.exp(math.log(4096.0) - 1.3862944 * jax.random.uniform(seeds[12], (MODEL_DIM, 2 * FF), jnp.float32) ** steps_of(seeds[12], (MODEL_DIM, 2 * FF), ((0, 32),), -0.2, 0.2)), 1024.0, 4096.0),
        "down_master": scatter_about(seeds[13], (FF, MODEL_DIM), FF ** -0.5, 0.0625, ((0, 32),), jnp.float32),
        "down_first": scatter_about(seeds[14], (FF, MODEL_DIM), (0.5 * (SEQUENCE_TOTAL * SEQUENCE_LENGTH) ** 0.5), 384.0, ((0, 32),), jnp.float32),
        "down_second": jnp.clip(jnp.exp(math.log(16384.0) - 1.3862944 * jax.random.uniform(seeds[15], (FF, MODEL_DIM), jnp.float32) ** steps_of(seeds[15], (FF, MODEL_DIM), ((0, 32),), -0.2, 0.2)), 4096.0, 16384.0),
        "gains_master": jnp.clip(1.0 + 0.1 * jax.random.normal(seeds[16], (2, MODEL_DIM), jnp.float32), 0.5, 1.5),
        "gains_first": scatter_about(seeds[17], (2, MODEL_DIM), ((SEQUENCE_TOTAL * SEQUENCE_LENGTH) ** 0.5), 768.0, ((1, 32),), jnp.float32),
        "gains_second": jnp.clip(jnp.exp(math.log(65536.0) - 1.3862944 * jax.random.uniform(seeds[18], (2, MODEL_DIM), jnp.float32) ** steps_of(seeds[18], (2, MODEL_DIM), ((1, 32),), -0.2, 0.2)), 16384.0, 65536.0),
    }


NORM_EPS = 1e-06
ROPE_BASE = 1000042.0
BETA_ONE = 0.5
BETA_TWO = 0.5
ADAM_EPS = 1e-08
DECAY_RATE = 0.1
GAIN_RATE = 0.3
OUT_RATE = 0.25
MASK_FILL = -1e+30
HIGHEST = lax.Precision.HIGHEST

@jax.custom_vjp
def low(v):
    return lax.optimization_barrier(v.astype(jnp.bfloat16)).astype(jnp.float32)

@jax.custom_vjp
def low_back(v):
    return v

def low_keep(v):
    return (low(v), None)

def low_pass(kept, grad):
    return (grad,)

def back_keep(v):
    return (v, None)

def back_low(kept, grad):
    return (low(grad),)
low.defvjp(low_keep, low_pass)
low_back.defvjp(back_keep, back_low)

def normalize(values, gain):
    return values * lax.rsqrt(lax.optimization_barrier(jnp.mean(values * values, axis=-1, keepdims=True)) + NORM_EPS) * gain

def angles_for(seq_positions, head_width):
    half_width = head_width // 2
    inverse_freq = jnp.exp(-jnp.log(ROPE_BASE) * (jnp.arange(half_width, dtype=jnp.float32) * 2.0 / head_width))
    return seq_positions.astype(jnp.float32)[..., None] * inverse_freq

def apply_rotary(values, rotary_angles):
    half_width = values.shape[-1] // 2
    cosine = jnp.cos(rotary_angles)[..., None, :]
    sine_part = jnp.sin(rotary_angles)[..., None, :]
    first_half = values[..., :half_width]
    second = values[..., half_width:]
    return jnp.concatenate([first_half * cosine - second * sine_part, second * cosine + first_half * sine_part], axis=-1)

def layer_forward(seq_inputs, seq_positions, length, lowered):
    qkv_w, out_w, gateup_w, down_w, gains = lowered
    sequence_length = seq_inputs.shape[0]
    group_width = QUERY_HEADS // KEY_VALUE_HEADS
    slot_ids = jnp.arange(sequence_length, dtype=jnp.int32)
    first_low = low(normalize(seq_inputs, gains[0]))
    projected_rows = low_back(jnp.dot(first_low, qkv_w, precision=HIGHEST))
    query_unrotated = projected_rows[:, :QUERY_HEADS * HEAD_DIM].reshape(sequence_length, QUERY_HEADS, HEAD_DIM)
    key_unrotated = projected_rows[:, QUERY_HEADS * HEAD_DIM:QUERY_HEADS * HEAD_DIM + KEY_VALUE_HEADS * HEAD_DIM].reshape(sequence_length, KEY_VALUE_HEADS, HEAD_DIM)
    value_unrotated = projected_rows[:, QUERY_HEADS * HEAD_DIM + KEY_VALUE_HEADS * HEAD_DIM:].reshape(sequence_length, KEY_VALUE_HEADS, HEAD_DIM)
    rotary_angles = angles_for(seq_positions, HEAD_DIM)
    query_heads_split = low(apply_rotary(query_unrotated, rotary_angles)).reshape(sequence_length, KEY_VALUE_HEADS, group_width, HEAD_DIM)
    key_heads = low(apply_rotary(key_unrotated, rotary_angles))
    value_heads = low(value_unrotated)
    scores = low_back(jnp.einsum('qngd,knd->ngqk', query_heads_split, key_heads, precision=HIGHEST) * HEAD_DIM ** (-0.5))
    allowed = (slot_ids[None, :] <= slot_ids[:, None]) & (slot_ids[None, :] < length)
    row_max = lax.optimization_barrier(jnp.max(jnp.where(allowed, scores, MASK_FILL), axis=-1, keepdims=True))
    weights_exp = jnp.exp(jnp.where(allowed, scores - row_max, MASK_FILL))
    probs_low = low(weights_exp / lax.optimization_barrier(jnp.sum(weights_exp, axis=-1, keepdims=True)))
    attended = jnp.einsum('ngqk,knd->qngd', probs_low, value_heads, precision=HIGHEST).reshape(sequence_length, QUERY_HEADS * HEAD_DIM)
    attended = low(low_back(attended))
    middle = seq_inputs + low_back(jnp.dot(attended, out_w, precision=HIGHEST))
    second_low = low(normalize(middle, gains[1]))
    gate_up = low_back(jnp.dot(second_low, gateup_w, precision=HIGHEST))
    mixed = low(jax.nn.silu(gate_up[:, :FF]) * gate_up[:, FF:])
    return middle + low_back(jnp.dot(mixed, down_w, precision=HIGHEST))

def adamw_update(master, first_moment, second_moment, gradient, step_rate):
    first_new = BETA_ONE * first_moment + (1.0 - BETA_ONE) * gradient
    second_new = BETA_TWO * second_moment + (1.0 - BETA_TWO) * gradient * gradient
    first_hat = first_new / (1.0 - BETA_ONE ** STEP)
    second_hat = second_new / (1.0 - BETA_TWO ** STEP)
    master_new = master - step_rate * (first_hat / (jnp.sqrt(second_hat) + ADAM_EPS) + DECAY_RATE * master)
    return (master_new, first_new, second_new, master_new.astype(jnp.bfloat16))

def reference(hidden, cotangent, lengths, positions, query_key_value_master, query_key_value_first, query_key_value_second, out_master, out_first, out_second, gateup_master, gateup_first, gateup_second, down_master, down_first, down_second, gains_master, gains_first, gains_second):
    masters = (query_key_value_master, out_master, gateup_master, down_master, gains_master)
    inputs = hidden.astype(jnp.float32)
    slot_ids = jnp.arange(SEQUENCE_LENGTH, dtype=jnp.int32)
    valid_rows = (slot_ids[None, :] < lengths[:, None]).astype(jnp.float32)
    checked = jax.checkpoint(layer_forward)

    def forward(params, layer_inputs):
        lowered = tuple((low(weight) for weight in params))

        def scan_step(loop_carry, seq_item):
            seq_inputs, seq_positions, length = seq_item
            return (loop_carry, checked(seq_inputs, seq_positions, length, lowered))
        _, results = lax.scan(scan_step, jnp.zeros((), jnp.float32), (layer_inputs, positions, lengths))
        return results
    output, pullback = jax.vjp(forward, masters, inputs)
    gradients, input_grad = pullback(cotangent.astype(jnp.float32) * valid_rows[..., None])
    qkv_grad, out_grad, gateup_grad, down_grad, gains_grad = gradients
    qkv_set = adamw_update(query_key_value_master, query_key_value_first, query_key_value_second, qkv_grad, MODEL_DIM ** (-0.5))
    out_set = adamw_update(out_master, out_first, out_second, out_grad, OUT_RATE)
    gateup_set = adamw_update(gateup_master, gateup_first, gateup_second, gateup_grad, MODEL_DIM ** (-0.5))
    down_set = adamw_update(down_master, down_first, down_second, down_grad, FF ** (-0.5))
    gains_set = adamw_update(gains_master, gains_first, gains_second, gains_grad, GAIN_RATE)
    return (output.astype(jnp.bfloat16), input_grad.astype(jnp.bfloat16), qkv_set[0], qkv_set[1], qkv_set[2], qkv_set[3], out_set[0], out_set[1], out_set[2], out_set[3], gateup_set[0], gateup_set[1], gateup_set[2], gateup_set[3], down_set[0], down_set[1], down_set[2], down_set[3], gains_set[0], gains_set[1], gains_set[2], gains_set[3])
```

```python
import jax
import jax.numpy as jnp
from jax import lax
from jax.sharding import Mesh
from jax.sharding import PartitionSpec as P

MODEL_DIM = 2048
QUERY_HEADS = 8
KEY_VALUE_HEADS = 4
HEAD_DIM = 256
FF = 8192
STEP = 10

NORM_EPS = 1e-06
ROPE_BASE = 1000042.0
BETA_ONE = 0.5
BETA_TWO = 0.5
ADAM_EPS = 1e-08
DECAY_RATE = 0.1
GAIN_RATE = 0.3
OUT_RATE = 0.25
MASK_FILL = -1e30

EVERY = ("s", "t", "p", "c")
DEPTH = ("s", "t")
PLANE = ("p", "c")
TEAM = ("t", "c")
LINE = ("s", "t", "c")
EXTRA = 128
DIGIT = 64

BF = jnp.bfloat16
F32 = jnp.float32


def normalize(values, gain):
    return values * lax.rsqrt(jnp.mean(values * values, axis=-1, keepdims=True) + NORM_EPS) * gain


def rotary_tables(seq_positions):
    half_width = HEAD_DIM // 2
    inverse_freq = jnp.exp(
        -jnp.log(ROPE_BASE) * (jnp.arange(half_width, dtype=F32) * 2.0 / HEAD_DIM)
    )
    angles = seq_positions.astype(F32)[..., None] * inverse_freq
    return jnp.cos(angles)[..., None, :], jnp.sin(angles)[..., None, :]


def rotate(values, cosine, sine):
    half_width = HEAD_DIM // 2
    first, second = values[..., :half_width], values[..., half_width:]
    return jnp.concatenate(
        [first * cosine - second * sine, second * cosine + first * sine], axis=-1
    )


def adamw_update(master, first_moment, second_moment, gradient, step_rate):
    first_new = BETA_ONE * first_moment + (1.0 - BETA_ONE) * gradient
    second_new = BETA_TWO * second_moment + (1.0 - BETA_TWO) * gradient * gradient
    first_hat = first_new / (1.0 - BETA_ONE**STEP)
    second_hat = second_new / (1.0 - BETA_TWO**STEP)
    master_new = master - step_rate * (
        first_hat / (jnp.sqrt(second_hat) + ADAM_EPS) + DECAY_RATE * master
    )
    return (master_new, first_new, second_new, master_new.astype(BF))


def pick(blocks, index):
    return lax.dynamic_index_in_dim(blocks, index, 0, keepdims=False)


def put(buffer, block, index):
    return lax.dynamic_update_index_in_dim(buffer, block, index, 0)


def exchange(blocks, axes):
    count = blocks.shape[0]
    me = lax.axis_index(axes)
    result = blocks
    for mask in range(1, count):
        pairs = [(source, source ^ mask) for source in range(count)]
        arrived = lax.ppermute(pick(blocks, me ^ mask), axes, pairs)
        result = put(result, arrived, me ^ mask)
    return result


def ring_gather(block, axes):
    count = lax.axis_size(axes)
    me = lax.axis_index(axes)
    half = block.shape[0] // 2
    result = jnp.zeros((count, 2, half) + block.shape[1:], block.dtype)
    ahead, behind = block[:half], block[half:]
    result = lax.dynamic_update_slice(result, ahead[None, None], (me, 0, 0, 0))
    result = lax.dynamic_update_slice(result, behind[None, None], (me, 1, 0, 0))
    up = [(source, (source + 1) % count) for source in range(count)]
    down = [(source, (source - 1) % count) for source in range(count)]
    for step in range(1, count):
        ahead = lax.ppermute(ahead, axes, up)
        behind = lax.ppermute(behind, axes, down)
        result = lax.dynamic_update_slice(
            result, ahead[None, None], ((me - step) % count, 0, 0, 0)
        )
        result = lax.dynamic_update_slice(
            result, behind[None, None], ((me + step) % count, 1, 0, 0)
        )
    return result.reshape((count * 2 * half,) + block.shape[1:])


def ring_order(depth, chips):
    if chips != 4:
        return list(range(depth * chips))
    order = []
    for level in range(depth):
        turn = (1, 3, 2) if level % 2 == 0 else (2, 3, 1)
        order += [level * chips + chip for chip in turn]
    return order + [level * chips for level in reversed(range(depth))]


def scatter_sum(term, order):
    devices = [2 * chip + core for chip in order for core in range(2)]
    return lax.psum_scatter(
        term, EVERY, scatter_dimension=0, axis_index_groups=[devices], tiled=True
    )


def in_ring_order(columns, order):
    width = columns.shape[1] // len(order)
    if order == list(range(len(order))):
        return columns
    return jnp.concatenate([columns[:, c * width : (c + 1) * width] for c in order], axis=1)


def shards(
    hidden,
    cotangent,
    lengths,
    positions,
    query_key_value_master,
    query_key_value_first,
    query_key_value_second,
    out_master,
    out_first,
    out_second,
    gateup_master,
    gateup_first,
    gateup_second,
    down_master,
    down_first,
    down_second,
    gains_master,
    gains_first,
    gains_second,
):
    members, block_length, width = hidden.shape
    depth = lax.axis_size(DEPTH)
    plane = lax.axis_size(PLANE)
    team = lax.axis_size(TEAM)
    line_count = lax.axis_size("s")
    team_chips = lax.axis_size("t")
    rows = members * block_length
    length_total = rows * team
    query_width = QUERY_HEADS * HEAD_DIM
    key_width = KEY_VALUE_HEADS * HEAD_DIM
    query_each = QUERY_HEADS // team
    key_each = KEY_VALUE_HEADS // team
    group = QUERY_HEADS // KEY_VALUE_HEADS
    score_scale = HEAD_DIM ** (-0.5)
    order = ring_order(depth, lax.axis_size("p"))

    rank = lax.axis_index(DEPTH)
    core = lax.axis_index("c")
    my_line = lax.axis_index("s")
    member_of_rank = rank % members

    gain_columns = jnp.pad(gains_master.astype(BF).T, ((0, 0), (0, EXTRA - 2)))
    qkv_ext = lax.all_gather(
        jnp.concatenate([query_key_value_master.astype(BF), gain_columns], axis=1),
        EVERY,
        axis=0,
        tiled=True,
    )
    out_w = lax.all_gather(out_master.astype(BF), EVERY, axis=0, tiled=True)
    qkv_w = qkv_ext[:, : query_width + 2 * key_width]
    gains = qkv_ext[:, query_width + 2 * key_width :][:, :2].astype(F32).T

    def flat_index(line, member):
        return (line * team_chips + member // 2) * 2 + member % 2

    def there_pairs(turn):
        pairs = []
        for r in range(depth):
            for k in range(2):
                i = (r % members + turn) % members
                pairs.append((2 * r + k, flat_index(k * members + i, r // members)))
        return pairs

    def to_sequence(blocks):
        arrived = []
        for turn in range(members):
            sent = pick(blocks, (member_of_rank + turn) % members)
            arrived.append(lax.ppermute(sent, LINE, there_pairs(turn)))
        result = jnp.stack(arrived)
        for turn in range(members):
            result = put(result, arrived[turn], (my_line % members - turn) % members)
        return result.reshape((rows,) + blocks.shape[2:])

    def from_sequence(values):
        blocks = values.reshape((members, block_length) + values.shape[1:])
        arrived = []
        for turn in range(members):
            sent = pick(blocks, (my_line % members - turn) % members)
            back = [(target, source) for source, target in there_pairs(turn)]
            arrived.append(lax.ppermute(sent, LINE, back))
        result = jnp.stack(arrived)
        for turn in range(members):
            result = put(result, arrived[turn], (member_of_rank + turn) % members)
        return result

    slot_ids = rank * block_length + jnp.arange(block_length, dtype=jnp.int32)
    valid = slot_ids[None, :] < lengths[:, None]
    spread = jnp.broadcast_to(lengths[:, None], positions.shape)
    digits = jnp.stack(
        [positions // DIGIT, positions % DIGIT, spread // DIGIT, spread % DIGIT], axis=-1
    ).astype(BF)
    digits = jnp.pad(digits, ((0, 0), (0, 0), (0, EXTRA - 4)))
    moved = to_sequence(jnp.concatenate([hidden, digits], axis=2))
    numbers = moved[:, width:][:, :4].astype(jnp.int32)
    my_positions = numbers[:, 0] * DIGIT + numbers[:, 1]
    my_length = numbers[0, 2] * DIGIT + numbers[0, 3]
    flat_inputs = moved[:, :width].astype(F32)

    ff_block = FF // (depth * plane)
    gateup_rows = gateup_master.shape[0]
    gateup_blocks = (
        gateup_master.astype(BF)
        .reshape(gateup_rows, 2, depth, plane, ff_block)
        .transpose(3, 0, 1, 2, 4)
        .reshape(plane, gateup_rows, 2 * depth * ff_block)
    )
    gateup_mine = exchange(gateup_blocks, PLANE).reshape(plane * gateup_rows, -1)
    gateup_w = ring_gather(gateup_mine, DEPTH)
    down_w = ring_gather(down_master.astype(BF), DEPTH)

    masked = jnp.where(valid[..., None], cotangent, jnp.zeros((), BF))
    out_back_low = to_sequence(masked)
    out_back_all = lax.all_gather(out_back_low, PLANE, axis=0, tiled=True)

    first_low = normalize(flat_inputs, gains[0]).astype(BF)
    projected = jnp.dot(first_low, qkv_w, preferred_element_type=F32)
    cosine, sine = rotary_tables(my_positions)
    query_part = rotate(
        projected[:, :query_width].reshape(rows, QUERY_HEADS, HEAD_DIM), cosine, sine
    ).astype(BF)
    key_part = rotate(
        projected[:, query_width : query_width + key_width].reshape(
            rows, KEY_VALUE_HEADS, HEAD_DIM
        ),
        cosine,
        sine,
    ).astype(BF)
    value_part = (
        projected[:, query_width + key_width :]
        .reshape(rows, KEY_VALUE_HEADS, HEAD_DIM)
        .astype(BF)
    )

    def heads_out(query_like, key_like, value_like):
        parts = [
            query_like.reshape(rows, team, query_each, HEAD_DIM),
            key_like.reshape(rows, team, key_each, HEAD_DIM),
            value_like.reshape(rows, team, key_each, HEAD_DIM),
        ]
        return exchange(jnp.concatenate(parts, axis=2).transpose(1, 2, 0, 3), TEAM)

    own_heads = (
        heads_out(query_part, key_part, value_part)
        .transpose(1, 0, 2, 3)
        .reshape(query_each + 2 * key_each, length_total, HEAD_DIM)
    )
    query_rows = own_heads[:query_each].reshape(key_each, group, length_total, HEAD_DIM)
    key_rows = own_heads[query_each : query_each + key_each]
    value_rows = own_heads[query_each + key_each :]
    slots = jnp.arange(length_total, dtype=jnp.int32)
    allowed = (slots[None, :] <= slots[:, None]) & (slots[None, :] < my_length)

    scores = (
        jnp.einsum("ngqd,nkd->ngqk", query_rows, key_rows, preferred_element_type=F32)
        * score_scale
    )
    row_max = jnp.max(jnp.where(allowed, scores, MASK_FILL), axis=-1, keepdims=True)
    weights_exp = jnp.exp(jnp.where(allowed, scores - row_max, MASK_FILL))
    row_sum = jnp.sum(weights_exp, axis=-1, keepdims=True)
    probs = weights_exp / row_sum
    probs_low = probs.astype(BF)
    attended_heads = jnp.einsum(
        "ngqk,nkd->ngqd", probs_low, value_rows, preferred_element_type=F32
    ).astype(BF)

    def heads_back(values, count):
        blocks = values.reshape(count, team, rows, HEAD_DIM).transpose(1, 0, 2, 3)
        return exchange(blocks, TEAM)

    attended_low = (
        heads_back(attended_heads.reshape(query_each, length_total, HEAD_DIM), query_each)
        .transpose(2, 0, 1, 3)
        .reshape(rows, query_width)
    )
    middle = flat_inputs + jnp.dot(attended_low, out_w, preferred_element_type=F32)
    second_low = normalize(middle, gains[1]).astype(BF)

    second_all = lax.all_gather(second_low, PLANE, axis=0, tiled=True)
    units = depth * ff_block
    gate_up = jnp.dot(second_all, gateup_w, preferred_element_type=F32)
    gate_part, up_part = gate_up[:, :units], gate_up[:, units:]
    sigmoid_gate = jax.nn.sigmoid(gate_part)
    silu_gate = gate_part * sigmoid_gate
    mixed_low = (silu_gate * up_part).astype(BF)
    branch_part = jnp.dot(mixed_low, down_w, preferred_element_type=F32).astype(BF)
    branch = lax.psum_scatter(branch_part, PLANE, scatter_dimension=0, tiled=True)
    output = from_sequence((middle + branch.astype(F32)).astype(BF))

    mixed_back = jnp.einsum("rk,ck->rc", out_back_all, down_w, preferred_element_type=F32)
    gate_back = mixed_back * up_part * sigmoid_gate * (1.0 + gate_part * (1.0 - sigmoid_gate))
    up_back = mixed_back * silu_gate
    gate_up_back = jnp.concatenate([gate_back, up_back], axis=1).astype(BF)
    norm_back_part = jnp.einsum(
        "rk,ck->rc", gate_up_back, gateup_w, preferred_element_type=F32
    ).astype(BF)
    norm_back = lax.psum_scatter(norm_back_part, PLANE, scatter_dimension=0, tiled=True)
    down_term = jnp.einsum(
        "rc,rk->ck", mixed_low, out_back_all, preferred_element_type=F32
    ).astype(BF)
    gateup_term = jnp.einsum(
        "rc,rk->ck", second_all, gate_up_back, preferred_element_type=F32
    ).astype(BF)
    down_grad = lax.psum_scatter(down_term, DEPTH, scatter_dimension=0, tiled=True)
    gateup_sum = lax.psum_scatter(gateup_term, DEPTH, scatter_dimension=0, tiled=True)
    gateup_grad = (
        exchange(gateup_sum.reshape(plane, gateup_rows, 2 * units), PLANE)
        .reshape(plane, gateup_rows, 2, depth, ff_block)
        .transpose(1, 2, 3, 0, 4)
        .reshape(gateup_rows, 2 * FF)
    )

    _, second_pull = jax.vjp(normalize, middle, gains[1])
    middle_norm_back, second_gain_grad = second_pull(norm_back.astype(F32))
    middle_back = out_back_low.astype(F32) + middle_norm_back
    branch_low = middle_back.astype(BF)
    out_term = jnp.einsum(
        "rc,rk->ck", in_ring_order(attended_low, order), branch_low, preferred_element_type=F32
    ).astype(BF)
    out_grad = scatter_sum(out_term, order)

    attended_back = jnp.einsum(
        "rk,ck->rc", branch_low, out_w, preferred_element_type=F32
    ).astype(BF)
    back_blocks = attended_back.reshape(rows, team, query_each, HEAD_DIM).transpose(1, 2, 0, 3)
    back_rows = (
        exchange(back_blocks, TEAM)
        .transpose(1, 0, 2, 3)
        .reshape(key_each, group, length_total, HEAD_DIM)
    )
    value_grad = jnp.einsum("ngqk,ngqd->nkd", probs_low, back_rows, preferred_element_type=F32)
    prob_back = jnp.einsum("ngqd,nkd->ngqk", back_rows, value_rows, preferred_element_type=F32)
    row_delta = jnp.sum(probs * prob_back, axis=-1, keepdims=True)
    score_back = (probs * (prob_back - row_delta)).astype(BF)
    query_grad = (
        jnp.einsum("ngqk,nkd->ngqd", score_back, key_rows, preferred_element_type=F32)
        * score_scale
    )
    key_grad = (
        jnp.einsum("ngqk,ngqd->nkd", score_back, query_rows, preferred_element_type=F32)
        * score_scale
    )
    head_grads = jnp.concatenate(
        [query_grad.reshape(query_each, length_total, HEAD_DIM), key_grad, value_grad], axis=0
    ).astype(BF)
    grads_back = heads_back(head_grads, query_each + 2 * key_each)
    query_back = grads_back[:, :query_each].transpose(2, 0, 1, 3).reshape(rows, QUERY_HEADS, -1)
    key_back = (
        grads_back[:, query_each : query_each + key_each]
        .transpose(2, 0, 1, 3)
        .reshape(rows, KEY_VALUE_HEADS, -1)
    )
    value_back = grads_back[:, query_each + key_each :].transpose(2, 0, 1, 3)
    projected_back = jnp.concatenate(
        [
            rotate(query_back.astype(F32), cosine, -sine).astype(BF).reshape(rows, query_width),
            rotate(key_back.astype(F32), cosine, -sine).astype(BF).reshape(rows, key_width),
            value_back.reshape(rows, key_width),
        ],
        axis=1,
    )
    first_back = jnp.einsum("rk,ck->rc", projected_back, qkv_w, preferred_element_type=F32)
    _, first_pull = jax.vjp(normalize, flat_inputs, gains[0])
    input_norm_back, first_gain_grad = first_pull(first_back)
    input_back = from_sequence((middle_back + input_norm_back).astype(BF))

    qkv_term = jnp.einsum(
        "rc,rk->ck", in_ring_order(first_low, order), projected_back, preferred_element_type=F32
    ).astype(BF)
    gain_terms = jnp.stack([first_gain_grad, second_gain_grad]).astype(BF)
    gain_terms = jnp.pad(in_ring_order(gain_terms, order).T, ((0, 0), (0, EXTRA - 2)))
    qkv_sum = scatter_sum(jnp.concatenate([qkv_term, gain_terms], axis=1), order)
    qkv_grad = qkv_sum[:, : query_width + 2 * key_width].astype(F32)
    gains_grad = qkv_sum[:, query_width + 2 * key_width :][:, :2].astype(F32).T

    qkv_set = adamw_update(
        query_key_value_master,
        query_key_value_first,
        query_key_value_second,
        qkv_grad,
        MODEL_DIM ** (-0.5),
    )
    out_set = adamw_update(out_master, out_first, out_second, out_grad.astype(F32), OUT_RATE)
    gateup_set = adamw_update(
        gateup_master,
        gateup_first,
        gateup_second,
        gateup_grad.astype(F32),
        MODEL_DIM ** (-0.5),
    )
    down_set = adamw_update(
        down_master, down_first, down_second, down_grad.astype(F32), FF ** (-0.5)
    )
    gains_set = adamw_update(gains_master, gains_first, gains_second, gains_grad, GAIN_RATE)
    return (
        (output, input_back) + qkv_set + out_set + gateup_set + down_set + gains_set
    )


def solution(mesh):
    ctx, fsdp = mesh.shape["ctx"], mesh.shape["fsdp"]
    line_count = 4
    fine = Mesh(mesh.devices.reshape(line_count, ctx // line_count, fsdp // 2, 2), EVERY)
    tokens = P(PLANE, DEPTH, None)
    weight = P(EVERY, None)
    gain = P(None, EVERY)
    return jax.shard_map(
        shards,
        mesh=fine,
        in_specs=(tokens, tokens, P(PLANE), P(PLANE, DEPTH)) + (weight,) * 12 + (gain,) * 3,
        out_specs=(tokens, tokens) + (weight,) * 16 + (gain,) * 4,
        check_vma=False,
    )
```

```python
import functools

import jax
import jax.numpy as jnp
from jax import lax
from jax.experimental import pallas as pl
from jax.experimental.pallas import tpu as pltpu
from jax.sharding import Mesh
from jax.sharding import PartitionSpec as P

MODEL_DIM = 2048
QUERY_HEADS = 8
KEY_VALUE_HEADS = 4
HEAD_DIM = 256
FF = 8192
STEP = 10

NORM_EPS = 1e-06
ROPE_BASE = 1000042.0
BETA_ONE = 0.5
BETA_TWO = 0.5
ADAM_EPS = 1e-08
DECAY_RATE = 0.1
GAIN_RATE = 0.3
OUT_RATE = 0.25
MASK_FILL = -1e30

EVERY = ("s", "t", "p", "c")
DEPTH = ("s", "t")
PLANE = ("p", "c")
TEAM = ("t", "c")
LINE = ("s", "t", "c")
EXTRA = 128
DIGIT = 64
CHUNKS = 2
VMEM_BYTES = 52 * 1024 * 1024

BF = jnp.bfloat16
F32 = jnp.float32


def normalize(values, gain):
    return values * lax.rsqrt(jnp.mean(values * values, axis=-1, keepdims=True) + NORM_EPS) * gain


def rotary_tables(seq_positions):
    half_width = HEAD_DIM // 2
    inverse_freq = jnp.exp(
        -jnp.log(ROPE_BASE) * (jnp.arange(half_width, dtype=F32) * 2.0 / HEAD_DIM)
    )
    angles = seq_positions.astype(F32)[..., None] * inverse_freq
    return jnp.cos(angles), jnp.sin(angles)


def rotate_heads(columns, cosine, sine):
    half = HEAD_DIM // 2
    parts = []
    for start in range(0, columns.shape[1], HEAD_DIM):
        first = columns[:, start : start + half]
        second = columns[:, start + half : start + HEAD_DIM]
        parts += [first * cosine - second * sine, second * cosine + first * sine]
    return parts


def adamw_update(master, first_moment, second_moment, gradient, step_rate):
    first_new = BETA_ONE * first_moment + (1.0 - BETA_ONE) * gradient
    second_new = BETA_TWO * second_moment + (1.0 - BETA_TWO) * gradient * gradient
    first_hat = first_new / (1.0 - BETA_ONE**STEP)
    second_hat = second_new / (1.0 - BETA_TWO**STEP)
    master_new = master - step_rate * (
        first_hat / (jnp.sqrt(second_hat) + ADAM_EPS) + DECAY_RATE * master
    )
    return (master_new, first_new, second_new, master_new.astype(BF))


def tie(*values):
    return lax.optimization_barrier(values)


def pick(blocks, index, axis=0):
    return lax.dynamic_index_in_dim(blocks, index, axis, keepdims=False)


def put(buffer, block, index):
    return lax.dynamic_update_index_in_dim(buffer, block, index, 0)


def swap(value, axes, mask):
    count = lax.axis_size(axes)
    return lax.ppermute(value, axes, [(source, source ^ mask) for source in range(count)])


def exchange(blocks, axes):
    me = lax.axis_index(axes)
    result = blocks
    for mask in range(1, blocks.shape[0]):
        result = put(result, swap(pick(blocks, me ^ mask), axes, mask), me ^ mask)
    return result


def sum_at_owner(chunk_of, axes):
    me = lax.axis_index(axes)
    total = chunk_of(me).astype(F32)
    for mask in range(1, lax.axis_size(axes)):
        total = total + swap(chunk_of(me ^ mask), axes, mask).astype(F32)
    return total


def ring_turn(state):
    ahead, behind = state
    count = lax.axis_size(DEPTH)
    up = [(source, (source + 1) % count) for source in range(count)]
    down = [(source, (source - 1) % count) for source in range(count)]
    return lax.ppermute(ahead, DEPTH, up), lax.ppermute(behind, DEPTH, down)


def pack_weights(gateup_part, down_part):
    columns = gateup_part.shape[1]
    halves = []
    for side in range(2):
        g, d = gateup_part.shape[0] // 2, down_part.shape[0] // 2
        rows = down_part[side * d : side * d + d]
        pieces = [rows[:, at : at + columns] for at in range(0, rows.shape[1], columns)]
        halves.append(
            jnp.concatenate([gateup_part[side * g : side * g + g]] + pieces, axis=0)
        )
    return tuple(halves)


def unpack_weights(states, gateup_part, down_part):
    count = lax.axis_size(DEPTH)
    me = lax.axis_index(DEPTH)
    columns = gateup_part.shape[1]
    g, d = gateup_part.shape[0] // 2, down_part.shape[0] // 2
    gateup = jnp.zeros((count, 2, g, columns), BF)
    down = jnp.zeros((count, 2, d, down_part.shape[1]), BF)
    for step, state in enumerate(states):
        for side in range(2):
            at = (me - step) % count if side == 0 else (me + step) % count
            gateup = lax.dynamic_update_slice(gateup, state[side][None, None, :g], (at, side, 0, 0))
            for n in range(down_part.shape[1] // columns):
                piece = state[side][None, None, g + n * d : g + n * d + d]
                down = lax.dynamic_update_slice(down, piece, (at, side, 0, n * columns))
    return gateup.reshape(-1, columns), down.reshape(-1, down_part.shape[1])


def ring_order(depth, chips):
    if chips != 4:
        return list(range(depth * chips))
    order = []
    for level in range(depth):
        turn = (1, 3, 2) if level % 2 == 0 else (2, 3, 1)
        order += [level * chips + chip for chip in turn]
    return order + [level * chips for level in reversed(range(depth))]


def scatter_sum(term, order):
    devices = [2 * chip + core for chip in order for core in range(2)]
    return lax.psum_scatter(
        term, EVERY, scatter_dimension=0, axis_index_groups=[devices], tiled=True
    )


def in_ring_order(columns, order):
    width = columns.shape[1] // len(order)
    if order == list(range(len(order))):
        return columns
    return jnp.concatenate([columns[:, c * width : (c + 1) * width] for c in order], axis=1)


NT = (((1,), (1,)), ((), ()))
TN = (((0,), (0,)), ((), ()))


def product(left, right, dims=(((1,), (0,)), ((), ()))):
    return lax.dot_general(left, right, dims, preferred_element_type=F32)


def allowed_keys(first_row, rows, span, length):
    row = first_row + lax.broadcasted_iota(jnp.int32, (rows, span), 0)
    key = lax.broadcasted_iota(jnp.int32, (rows, span), 1)
    return (key <= row) & (key < length)


def attend_kernel(length_ref, query_ref, key_ref, value_ref, out_ref, total_ref, *, block):
    length = length_ref[0]
    for start in range(0, query_ref.shape[0], block):
        span = start + block
        query = query_ref[start:span, :]
        scores = product(query, key_ref[:span, :], NT) * (HEAD_DIM ** (-0.5))
        allowed = allowed_keys(start, block, span, length)
        scores = jnp.where(allowed, scores, MASK_FILL)
        row_max = jnp.max(scores, axis=1, keepdims=True)
        weights = jnp.where(allowed, jnp.exp(scores - row_max), 0.0)
        row_sum = jnp.sum(weights, axis=1, keepdims=True)
        probs = (weights * (1.0 / row_sum)).astype(BF)
        out_ref[start:span, :] = product(probs, value_ref[:span, :]).astype(BF)
        total_ref[0, start:span, :] = row_max + jnp.log(row_sum)


def attend_back_kernel(
    length_ref,
    query_ref,
    key_ref,
    value_ref,
    back_ref,
    total_ref,
    query_grad_ref,
    key_grad_ref,
    value_grad_ref,
    key_sum,
    value_sum,
    *,
    block,
    group,
):
    length = length_ref[0]
    scale = HEAD_DIM ** (-0.5)
    key_sum[...] = jnp.zeros_like(key_sum)
    value_sum[...] = jnp.zeros_like(value_sum)
    for head in range(group):
        columns = slice(head * HEAD_DIM, (head + 1) * HEAD_DIM)
        for start in range(0, query_ref.shape[0], block):
            span = start + block
            query = query_ref[start:span, columns]
            back = back_ref[start:span, columns]
            key, value = key_ref[:span, :], value_ref[:span, :]
            scores = product(query, key, NT) * scale
            allowed = allowed_keys(start, block, span, length)
            shifted = jnp.where(allowed, scores - total_ref[head, start:span, :], MASK_FILL)
            probs = jnp.exp(shifted)
            prob_back = product(back, value, NT)
            delta = jnp.sum(probs * prob_back, axis=1, keepdims=True)
            score_back = (probs * (prob_back - delta)).astype(BF)
            query_grad_ref[start:span, columns] = (product(score_back, key) * scale).astype(BF)
            key_sum[:span, :] += product(score_back, query, TN)
            value_sum[:span, :] += product(probs.astype(BF), back, TN)
    key_grad_ref[...] = (key_sum[...] * scale).astype(BF)
    value_grad_ref[...] = value_sum[...].astype(BF)


def attend(length, heads, query_each, key_each):
    slots = heads.shape[0]
    group = query_each // key_each
    block = min(256, slots)
    flops = 4 * query_each * slots * slots * HEAD_DIM // 2
    return pl.pallas_call(
        functools.partial(attend_kernel, block=block),
        grid=(query_each,),
        in_specs=[
            pl.BlockSpec(memory_space=pltpu.SMEM),
            pl.BlockSpec((slots, HEAD_DIM), lambda h: (0, h)),
            pl.BlockSpec((slots, HEAD_DIM), lambda h: (0, query_each + h // group)),
            pl.BlockSpec((slots, HEAD_DIM), lambda h: (0, query_each + key_each + h // group)),
        ],
        out_specs=[
            pl.BlockSpec((slots, HEAD_DIM), lambda h: (0, h)),
            pl.BlockSpec((1, slots, 1), lambda h: (h, 0, 0)),
        ],
        out_shape=[
            jax.ShapeDtypeStruct((slots, query_each * HEAD_DIM), BF),
            jax.ShapeDtypeStruct((query_each, slots, 1), F32),
        ],
        compiler_params=pltpu.CompilerParams(vmem_limit_bytes=VMEM_BYTES),
        cost_estimate=pl.CostEstimate(
            flops=flops, bytes_accessed=heads.size * 3, transcendentals=slots * slots
        ),
    )(length, heads, heads, heads)


def attend_back(length, heads, back, total, query_each, key_each):
    slots = heads.shape[0]
    group = query_each // key_each
    block = min(256, slots)
    flops = 10 * query_each * slots * slots * HEAD_DIM // 2
    return pl.pallas_call(
        functools.partial(attend_back_kernel, block=block, group=group),
        grid=(key_each,),
        in_specs=[
            pl.BlockSpec(memory_space=pltpu.SMEM),
            pl.BlockSpec((slots, group * HEAD_DIM), lambda n: (0, n)),
            pl.BlockSpec((slots, HEAD_DIM), lambda n: (0, query_each + n)),
            pl.BlockSpec((slots, HEAD_DIM), lambda n: (0, query_each + key_each + n)),
            pl.BlockSpec((slots, group * HEAD_DIM), lambda n: (0, n)),
            pl.BlockSpec((group, slots, 1), lambda n: (n, 0, 0)),
        ],
        out_specs=[
            pl.BlockSpec((slots, group * HEAD_DIM), lambda n: (0, n)),
            pl.BlockSpec((slots, HEAD_DIM), lambda n: (0, n)),
            pl.BlockSpec((slots, HEAD_DIM), lambda n: (0, n)),
        ],
        out_shape=[
            jax.ShapeDtypeStruct((slots, query_each * HEAD_DIM), BF),
            jax.ShapeDtypeStruct((slots, key_each * HEAD_DIM), BF),
            jax.ShapeDtypeStruct((slots, key_each * HEAD_DIM), BF),
        ],
        scratch_shapes=[pltpu.VMEM((slots, HEAD_DIM), F32), pltpu.VMEM((slots, HEAD_DIM), F32)],
        compiler_params=pltpu.CompilerParams(vmem_limit_bytes=VMEM_BYTES),
        cost_estimate=pl.CostEstimate(
            flops=flops, bytes_accessed=heads.size * 6, transcendentals=slots * slots * 2
        ),
    )(length, heads, heads, heads, back, total)


def feed_kernel(*refs, tiles, units, first, last, names):
    r = dict(zip(names, refs))
    mine = pl.program_id(0) < tiles
    if first:
        second = jnp.where(mine, r["c_own"][...], r["c_oth"][...])
        back = jnp.where(mine, r["d_own"][...], r["d_oth"][...])
        r["c_all"][...] = second
        r["d_all"][...] = back
    else:
        second, back = r["c_in"][...], r["d_in"][...]
    gate_up = product(second, r["gateup"][...])
    gate, up = gate_up[:, :units], gate_up[:, units:]
    sigmoid = 1.0 / (1.0 + jnp.exp(-gate))
    silu = gate * sigmoid
    mixed = (silu * up).astype(BF)
    r["mixed"][...] = mixed
    mixed_back = product(back, r["down"][...], NT)
    gate_back = mixed_back * up * sigmoid * (1.0 + gate * (1.0 - sigmoid))
    both = jnp.concatenate([gate_back, mixed_back * silu], axis=1).astype(BF)
    r["dr"][...] = both
    branch = product(mixed, r["down"][...])
    norm_back = product(both, r["gateup"][...], NT)
    if not first:
        branch = branch + r["o_in"][...].astype(F32)
        norm_back = norm_back + r["n_in"][...].astype(F32)
    branch, norm_back = branch.astype(BF), norm_back.astype(BF)
    if not last:
        r["o_part"][...] = branch
        r["n_part"][...] = norm_back
    else:

        @pl.when(mine)
        def _():
            r["o_own"][...] = branch
            r["n_own"][...] = norm_back

        @pl.when(jnp.logical_not(mine))
        def _():
            r["o_oth"][...] = branch
            r["n_oth"][...] = norm_back


def feed(chunk, block, blocks, gateup, down, tokens, partial, kept):
    first, last = chunk == 0, chunk == CHUNKS - 1
    width, two_units = gateup.shape
    units = two_units // 2
    if first:
        rows = tokens[0].shape[0]
    else:
        rows = partial[0].shape[0] // 2
    tile = min(256, rows)
    tiles = rows // tile
    whole = blocks * 2 * rows
    offset = block * 2 * tiles
    own = pl.BlockSpec((tile, width), lambda t: (jnp.minimum(t, tiles - 1), 0))
    oth = pl.BlockSpec((tile, width), lambda t: (jnp.maximum(t - tiles, 0), 0))
    here = pl.BlockSpec((tile, width), lambda t: (offset + t, 0))
    plain = pl.BlockSpec((tile, width), lambda t: (t, 0))
    once = pl.Buffered(1)
    names, operands, in_specs = [], [], []

    def give(name, value, spec):
        names.append(name)
        operands.append(value)
        in_specs.append(spec)

    if first:
        for name, value, spec in zip(("c_own", "c_oth", "d_own", "d_oth"), tokens, (own, oth) * 2):
            give(name, value, spec)
    else:
        give("c_in", kept["c_all"], here)
        give("d_in", kept["d_all"], here)
        give("o_in", partial[0], plain)
        give("n_in", partial[1], plain)
    give("gateup", gateup, pl.BlockSpec((width, two_units), lambda t: (0, 0), pipeline_mode=once))
    give("down", down, pl.BlockSpec((units, width), lambda t: (0, 0), pipeline_mode=once))
    outs, out_specs, shapes = [], [], []

    def take(name, shape, spec):
        outs.append(name)
        out_specs.append(spec)
        shapes.append(jax.ShapeDtypeStruct(shape, BF))

    if last:
        for name, spec in zip(("o_own", "o_oth", "n_own", "n_oth"), (own, oth) * 2):
            take(name, (rows, width), spec)
    else:
        take("o_part", (2 * rows, width), plain)
        take("n_part", (2 * rows, width), plain)
    aliases = {}
    held = [("mixed", units, CHUNKS * units), ("dr", two_units, CHUNKS * two_units)]
    if first:
        held += [("c_all", width, width), ("d_all", width, width)]
    for name, columns, total in held:
        if name in kept:
            aliases[len(operands)] = len(outs)
            give(name + "_kept", kept[name], pl.BlockSpec(memory_space=pl.ANY))
        at = 0 if total == columns else chunk
        take(
            name,
            (whole, total),
            pl.BlockSpec((tile, columns), lambda t, at=at: (offset + t, at)),
        )
    results = pl.pallas_call(
        functools.partial(
            feed_kernel,
            tiles=tiles,
            units=units,
            first=first,
            last=last,
            names=names + outs,
        ),
        grid=(2 * tiles,),
        in_specs=in_specs,
        out_specs=out_specs,
        out_shape=shapes,
        input_output_aliases=aliases,
        compiler_params=pltpu.CompilerParams(vmem_limit_bytes=VMEM_BYTES),
        cost_estimate=pl.CostEstimate(
            flops=2 * 2 * rows * width * 3 * two_units,
            bytes_accessed=2 * 2 * rows * width * 8,
            transcendentals=2 * rows * units,
        ),
    )(*operands)
    got = dict(zip(outs, results))
    for name, _, _ in held:
        kept[name] = got[name]
    return got


def shards(
    hidden,
    cotangent,
    lengths,
    positions,
    query_key_value_master,
    query_key_value_first,
    query_key_value_second,
    out_master,
    out_first,
    out_second,
    gateup_master,
    gateup_first,
    gateup_second,
    down_master,
    down_first,
    down_second,
    gains_master,
    gains_first,
    gains_second,
):
    members, block_length, width = hidden.shape
    depth = lax.axis_size(DEPTH)
    plane = lax.axis_size(PLANE)
    team = lax.axis_size(TEAM)
    team_chips = lax.axis_size("t")
    rows = members * block_length
    length_total = rows * team
    query_width = QUERY_HEADS * HEAD_DIM
    key_width = KEY_VALUE_HEADS * HEAD_DIM
    query_each = QUERY_HEADS // team
    key_each = KEY_VALUE_HEADS // team
    chips = lax.axis_size("p")
    order = ring_order(depth, chips)

    rank = lax.axis_index(DEPTH)
    my_line = lax.axis_index("s")
    member_of_rank = rank % members

    gain_columns = jnp.pad(gains_master.astype(BF).T, ((0, 0), (0, EXTRA - 2)))
    qkv_ext = lax.all_gather(
        jnp.concatenate([query_key_value_master.astype(BF), gain_columns], axis=1),
        EVERY,
        axis=0,
        tiled=True,
    )
    out_w = lax.all_gather(out_master.astype(BF), EVERY, axis=0, tiled=True)

    def flat_index(line, member):
        return (line * team_chips + member // 2) * 2 + member % 2

    def there_pairs(turn):
        pairs = []
        for r in range(depth):
            for k in range(2):
                i = (r % members + turn) % members
                pairs.append((2 * r + k, flat_index(k * members + i, r // members)))
        return pairs

    def to_sequence(blocks):
        arrived = []
        for turn in range(members):
            sent = pick(blocks, (member_of_rank + turn) % members)
            arrived.append(lax.ppermute(sent, LINE, there_pairs(turn)))
        result = jnp.stack(arrived)
        for turn in range(members):
            result = put(result, arrived[turn], (my_line % members - turn) % members)
        return result.reshape((rows,) + blocks.shape[2:])

    def from_sequence(values):
        blocks = values.reshape((members, block_length) + values.shape[1:])
        arrived = []
        for turn in range(members):
            sent = pick(blocks, (my_line % members - turn) % members)
            back = [(target, source) for source, target in there_pairs(turn)]
            arrived.append(lax.ppermute(sent, LINE, back))
        result = jnp.stack(arrived)
        for turn in range(members):
            result = put(result, arrived[turn], (member_of_rank + turn) % members)
        return result

    slot_ids = rank * block_length + jnp.arange(block_length, dtype=jnp.int32)
    valid = slot_ids[None, :] < lengths[:, None]
    spread = jnp.broadcast_to(lengths[:, None], positions.shape)
    digits = jnp.stack(
        [positions // DIGIT, positions % DIGIT, spread // DIGIT, spread % DIGIT], axis=-1
    ).astype(BF)
    digits = jnp.pad(digits, ((0, 0), (0, 0), (0, EXTRA - 4)))
    moved = to_sequence(jnp.concatenate([hidden, digits], axis=2))
    masked = jnp.where(valid[..., None], cotangent, jnp.zeros((), BF))

    ff_block = FF // (depth * plane * CHUNKS)
    gateup_rows = gateup_master.shape[0]
    chunk_width = 2 * depth * ff_block
    gateup_blocks = (
        gateup_master.astype(BF)
        .reshape(gateup_rows, 2, depth, plane, CHUNKS, ff_block)
        .transpose(3, 0, 4, 1, 2, 5)
        .reshape(plane, gateup_rows, CHUNKS * chunk_width)
    )
    gateup_mine = exchange(gateup_blocks, PLANE).reshape(plane * gateup_rows, -1)
    gateup_mine, moved = tie(gateup_mine, moved)
    down_low = down_master.astype(BF)
    parts = [
        (
            gateup_mine[:, n * chunk_width : (n + 1) * chunk_width],
            down_low[n * ff_block : (n + 1) * ff_block],
        )
        for n in range(CHUNKS)
    ]
    rings = [[pack_weights(*part)] for part in parts]
    turns = [(n, step) for n in range(CHUNKS) for step in range(1, depth)]

    def turn_on(count):
        done = []
        for n, _ in turns[:count]:
            rings[n].append(ring_turn(rings[n][-1]))
            done.append(n)
        del turns[:count]
        return done

    def settle(done, *values):
        flat = []
        for n in done:
            flat += list(rings[n][-1])
        got = tie(*flat, *values)
        for place, n in enumerate(done):
            rings[n][-1] = (got[2 * place], got[2 * place + 1])
        return got[2 * len(done) :]

    moved, masked = settle(turn_on(1), moved, masked)
    out_back_low = to_sequence(masked)
    qkv_ext, moved, out_back_low = settle(turn_on(1), qkv_ext, moved, out_back_low)

    numbers = moved[:, width:][:, :4].astype(jnp.int32)
    my_positions = numbers[:, 0] * DIGIT + numbers[:, 1]
    my_length = (numbers[0, 2] * DIGIT + numbers[0, 3]).reshape(1)
    flat_inputs = moved[:, :width].astype(F32)
    qkv_w = qkv_ext[:, : query_width + 2 * key_width]
    gains = qkv_ext[:, query_width + 2 * key_width :][:, :2].astype(F32).T
    first_low = normalize(flat_inputs, gains[0]).astype(BF)
    projected = jnp.dot(first_low, qkv_w, preferred_element_type=F32)
    cosine, sine = rotary_tables(my_positions)
    members_of_team = []
    for u in range(team):
        query = projected[:, u * query_each * HEAD_DIM : (u + 1) * query_each * HEAD_DIM]
        at = query_width + u * key_each * HEAD_DIM
        key = projected[:, at : at + key_each * HEAD_DIM]
        value = projected[:, at + key_width : at + key_width + key_each * HEAD_DIM]
        members_of_team.append(
            jnp.concatenate(
                rotate_heads(query, cosine, sine) + rotate_heads(key, cosine, sine) + [value],
                axis=1,
            ).astype(BF)
        )
    heads = exchange(jnp.stack(members_of_team), TEAM).reshape(length_total, -1)
    (heads,) = settle(turn_on(1), heads)

    half = rows // 2
    relay = chips == 4

    def fan_out(value):
        masks = (1, 2) if relay else range(1, chips)
        return {mask: swap(value, "p", mask) for mask in masks}

    def pass_on(held):
        return [swap(held[1][:half], "p", 2), swap(held[2][half:], "p", 1)]

    dy = fan_out(out_back_low)
    dy_cross = {0: swap(out_back_low, "c", 1)}
    attended_heads, log_total = attend(my_length, heads, query_each, key_each)
    attended_parts = exchange(attended_heads.reshape(team, rows, -1), TEAM)
    (attended_parts,) = settle(turn_on(1), attended_parts)
    attended_low = jnp.concatenate([attended_parts[u] for u in range(team)], axis=1)
    middle = flat_inputs + jnp.dot(attended_low, out_w, preferred_element_type=F32)
    second_low = normalize(middle, gains[1]).astype(BF)
    keys = sorted(dy)
    got = settle(turn_on(1), second_low, dy_cross[0], *[dy[m] for m in keys])
    second_low, dy_cross[0] = got[:2]
    dy = dict(zip(keys, got[2:]))

    weights = {0: unpack_weights(rings[0], *parts[0])}
    cs = fan_out(second_low)
    cs_cross = {0: swap(second_low, "c", 1)}
    kept = {}
    partials = {}

    def run(chunk, block, tokens):
        got = feed(chunk, block, chips, *weights[chunk], tokens, partials.get(block), kept)
        if chunk < CHUNKS - 1:
            partials[block] = (got["o_part"], got["n_part"])
        return got

    dy_halves = pass_on(dy) if relay else []
    for mask in keys:
        dy_cross[mask] = swap(dy[mask], "c", 1)
    results = {}
    results[0] = run(0, 0, (second_low, cs_cross[0], out_back_low, dy_cross[0]))
    names = ("mixed", "dr", "c_all", "d_all")
    flat = [cs[m] for m in keys] + [dy_cross[m] for m in keys] + dy_halves
    got = settle(turn_on(1), *[kept[n] for n in names], *flat)
    kept.update(zip(names, got[:4]))
    got = got[4:]
    cs = dict(zip(keys, got))
    dy_cross.update(zip(keys, got[len(keys) :]))
    dy_halves = got[2 * len(keys) :]
    cs_halves = pass_on(cs) if relay else []
    if relay:
        dy[3] = jnp.concatenate(dy_halves, axis=0)
        dy_cross[3] = swap(dy[3], "c", 1)
    for mask in keys:
        cs_cross[mask] = swap(cs[mask], "c", 1)
    for mask in keys:
        results[mask] = run(0, mask, (cs[mask], cs_cross[mask], dy[mask], dy_cross[mask]))
    if relay:
        got = tie(*[kept[n] for n in names], *cs_halves)
        kept.update(zip(names, got[:4]))
        cs[3] = jnp.concatenate(got[4:], axis=0)
        cs_cross[3] = swap(cs[3], "c", 1)
        results[3] = run(0, 3, (cs[3], cs_cross[3], dy[3], dy_cross[3]))
    settle(turn_on(len(turns)))
    for chunk in range(1, CHUNKS):
        weights[chunk] = unpack_weights(rings[chunk], *parts[chunk])

    def chip_sum(own, other):
        return (own.astype(F32) + swap(other, "c", 1).astype(F32)).astype(BF)

    norm_sums = {}
    for chunk in range(1, CHUNKS):
        for mask in (3, 1, 2, 0) if relay else range(chips):
            results[mask] = run(chunk, mask, None)
            if chunk == CHUNKS - 1:
                norm_sums[mask] = chip_sum(results[mask]["n_own"], results[mask]["n_oth"])
                if mask:
                    norm_sums[mask] = swap(norm_sums[mask], "p", mask)
    if CHUNKS == 1:
        for mask in range(chips):
            norm_sums[mask] = chip_sum(results[mask]["n_own"], results[mask]["n_oth"])
            if mask:
                norm_sums[mask] = swap(norm_sums[mask], "p", mask)

    down_term = jnp.einsum(
        "rc,rk->ck", kept["mixed"], kept["d_all"], preferred_element_type=F32
    ).astype(BF)
    gateup_term = jnp.einsum(
        "rc,rk->ck", kept["c_all"], kept["dr"], preferred_element_type=F32
    ).astype(BF)
    norm_back = norm_sums[0].astype(F32)
    for mask in range(1, chips):
        norm_back = norm_back + norm_sums[mask].astype(F32)

    branch_own = [results[mask]["o_own"] for mask in range(chips)]
    branch_oth = [results[mask]["o_oth"] for mask in range(chips)]
    got = tie(norm_sums[0], *branch_own, *branch_oth)
    branch_own, branch_oth = got[1 : 1 + chips], got[1 + chips :]
    branch = chip_sum(branch_own[0], branch_oth[0]).astype(F32)
    for mask in range(1, chips):
        branch = branch + swap(chip_sum(branch_own[mask], branch_oth[mask]), "p", mask).astype(F32)
    output = from_sequence((middle + branch).astype(BF))

    gateup_chunks = gateup_term.reshape(depth, plane * gateup_rows, CHUNKS * chunk_width)
    down_chunks = down_term.reshape(CHUNKS, depth, ff_block, width)
    gateup_sum = sum_at_owner(lambda z: pick(gateup_chunks, z), DEPTH).astype(BF)
    down_grad = sum_at_owner(
        lambda z: pick(down_chunks, z, 1).reshape(CHUNKS * ff_block, width), DEPTH
    )
    gateup_grad = (
        exchange(gateup_sum.reshape(plane, gateup_rows, CHUNKS * chunk_width), PLANE)
        .reshape(plane, gateup_rows, CHUNKS, 2, depth, ff_block)
        .transpose(1, 3, 4, 0, 2, 5)
        .reshape(gateup_rows, 2 * FF)
    )

    _, second_pull = jax.vjp(normalize, middle, gains[1])
    middle_norm_back, second_gain_grad = second_pull(norm_back)
    middle_back = out_back_low.astype(F32) + middle_norm_back
    branch_low = middle_back.astype(BF)

    attended_back = jnp.einsum(
        "rk,ck->rc", branch_low, out_w, preferred_element_type=F32
    ).astype(BF)
    group_width = query_each * HEAD_DIM
    back_blocks = jnp.stack(
        [attended_back[:, u * group_width : (u + 1) * group_width] for u in range(team)]
    )
    back_rows = exchange(back_blocks, TEAM).reshape(length_total, group_width)
    out_term = jnp.einsum(
        "rc,rk->ck", in_ring_order(attended_low, order), branch_low, preferred_element_type=F32
    ).astype(BF)
    out_grad = scatter_sum(out_term, order)
    head_grads = attend_back(my_length, heads, back_rows, log_total, query_each, key_each)
    query_back, key_back, value_back = [
        exchange(grad.reshape(team, rows, -1), TEAM) for grad in head_grads
    ]
    columns = []
    for back in (query_back, key_back):
        for u in range(team):
            columns += rotate_heads(back[u].astype(F32), cosine, -sine)
    columns = [part.astype(BF) for part in columns] + [value_back[u] for u in range(team)]
    projected_back = jnp.concatenate(columns, axis=1)
    first_back = jnp.einsum("rk,ck->rc", projected_back, qkv_w, preferred_element_type=F32)
    _, first_pull = jax.vjp(normalize, flat_inputs, gains[0])
    input_norm_back, first_gain_grad = first_pull(first_back)
    input_back = from_sequence((middle_back + input_norm_back).astype(BF))

    qkv_term = jnp.einsum(
        "rc,rk->ck", in_ring_order(first_low, order), projected_back, preferred_element_type=F32
    ).astype(BF)
    gain_terms = jnp.stack([first_gain_grad, second_gain_grad]).astype(BF)
    gain_terms = jnp.pad(in_ring_order(gain_terms, order).T, ((0, 0), (0, EXTRA - 2)))
    qkv_sum = scatter_sum(jnp.concatenate([qkv_term, gain_terms], axis=1), order)
    qkv_grad = qkv_sum[:, : query_width + 2 * key_width].astype(F32)
    gains_grad = qkv_sum[:, query_width + 2 * key_width :][:, :2].astype(F32).T

    qkv_set = adamw_update(
        query_key_value_master,
        query_key_value_first,
        query_key_value_second,
        qkv_grad,
        MODEL_DIM ** (-0.5),
    )
    out_set = adamw_update(out_master, out_first, out_second, out_grad.astype(F32), OUT_RATE)
    gateup_set = adamw_update(
        gateup_master,
        gateup_first,
        gateup_second,
        gateup_grad.astype(F32),
        MODEL_DIM ** (-0.5),
    )
    down_set = adamw_update(
        down_master, down_first, down_second, down_grad, FF ** (-0.5)
    )
    gains_set = adamw_update(gains_master, gains_first, gains_second, gains_grad, GAIN_RATE)
    return (
        (output, input_back) + qkv_set + out_set + gateup_set + down_set + gains_set
    )


def solution(mesh):
    ctx, fsdp = mesh.shape["ctx"], mesh.shape["fsdp"]
    line_count = 4
    fine = Mesh(mesh.devices.reshape(line_count, ctx // line_count, fsdp // 2, 2), EVERY)
    tokens = P(PLANE, DEPTH, None)
    weight = P(EVERY, None)
    gain = P(None, EVERY)
    return jax.shard_map(
        shards,
        mesh=fine,
        in_specs=(tokens, tokens, P(PLANE), P(PLANE, DEPTH)) + (weight,) * 12 + (gain,) * 3,
        out_specs=(tokens, tokens) + (weight,) * 16 + (gain,) * 4,
        check_vma=False,
    )
```

```python
import functools

import jax
import jax.numpy as jnp
from jax import lax
from jax.experimental import pallas as pl
from jax.experimental.pallas import tpu as pltpu
from jax.sharding import Mesh
from jax.sharding import PartitionSpec as P

MODEL_DIM = 2048
QUERY_HEADS = 8
KEY_VALUE_HEADS = 4
HEAD_DIM = 256
FF = 8192
STEP = 10

NORM_EPS = 1e-06
ROPE_BASE = 1000042.0
BETA_ONE = 0.5
BETA_TWO = 0.5
ADAM_EPS = 1e-08
DECAY_RATE = 0.1
GAIN_RATE = 0.3
OUT_RATE = 0.25
MASK_FILL = -1e30

EVERY = ("s", "t", "p", "c")
DEPTH = ("s", "t")
PLANE = ("p", "c")
TEAM = ("t", "c")
LINE = ("s", "t", "c")
EXTRA = 128
DIGIT = 64
CHUNKS = 2
VMEM_BYTES = 52 * 1024 * 1024

BF = jnp.bfloat16
F32 = jnp.float32


def normalize(values, gain):
    return values * lax.rsqrt(jnp.mean(values * values, axis=-1, keepdims=True) + NORM_EPS) * gain


def rotary_tables(seq_positions):
    half_width = HEAD_DIM // 2
    inverse_freq = jnp.exp(
        -jnp.log(ROPE_BASE) * (jnp.arange(half_width, dtype=F32) * 2.0 / HEAD_DIM)
    )
    angles = seq_positions.astype(F32)[..., None] * inverse_freq
    return jnp.cos(angles), jnp.sin(angles)


def rotate_heads(columns, cosine, sine):
    half = HEAD_DIM // 2
    parts = []
    for start in range(0, columns.shape[1], HEAD_DIM):
        first = columns[:, start : start + half]
        second = columns[:, start + half : start + HEAD_DIM]
        parts += [first * cosine - second * sine, second * cosine + first * sine]
    return parts


def adamw_update(master, first_moment, second_moment, gradient, step_rate):
    first_new = BETA_ONE * first_moment + (1.0 - BETA_ONE) * gradient
    second_new = BETA_TWO * second_moment + (1.0 - BETA_TWO) * gradient * gradient
    first_hat = first_new / (1.0 - BETA_ONE**STEP)
    second_hat = second_new / (1.0 - BETA_TWO**STEP)
    master_new = master - step_rate * (
        first_hat / (jnp.sqrt(second_hat) + ADAM_EPS) + DECAY_RATE * master
    )
    return (master_new, first_new, second_new, master_new.astype(BF))


def tie(*values):
    return lax.optimization_barrier(values)


def pick(blocks, index, axis=0):
    return lax.dynamic_index_in_dim(blocks, index, axis, keepdims=False)


def put(buffer, block, index):
    return lax.dynamic_update_index_in_dim(buffer, block, index, 0)


def swap(value, axes, mask):
    count = lax.axis_size(axes)
    return lax.ppermute(value, axes, [(source, source ^ mask) for source in range(count)])


def exchange(blocks, axes):
    me = lax.axis_index(axes)
    result = blocks
    for mask in range(1, blocks.shape[0]):
        result = put(result, swap(pick(blocks, me ^ mask), axes, mask), me ^ mask)
    return result


def total_of(terms):
    total = terms[0].astype(F32)
    for term in terms[1:]:
        total = total + term.astype(F32)
    return total


def depth_gather(block):
    me = lax.axis_index(DEPTH)
    count = lax.axis_size(DEPTH)
    result = put(jnp.zeros((count,) + block.shape, block.dtype), block, me)
    for mask in range(1, count):
        result = put(result, swap(block, DEPTH, mask), me ^ mask)
    return result


def ring_turn(state):
    ahead, behind = state
    count = lax.axis_size(DEPTH)
    up = [(source, (source + 1) % count) for source in range(count)]
    down = [(source, (source - 1) % count) for source in range(count)]
    return lax.ppermute(ahead, DEPTH, up), lax.ppermute(behind, DEPTH, down)


def pack_weights(gateup_part, down_part):
    columns = gateup_part.shape[1]
    halves = []
    for side in range(2):
        g, d = gateup_part.shape[0] // 2, down_part.shape[0] // 2
        rows = down_part[side * d : side * d + d]
        pieces = [rows[:, at : at + columns] for at in range(0, rows.shape[1], columns)]
        halves.append(
            jnp.concatenate([gateup_part[side * g : side * g + g]] + pieces, axis=0)
        )
    return tuple(halves)


def unpack_weights(states, gateup_part, down_part):
    count = lax.axis_size(DEPTH)
    me = lax.axis_index(DEPTH)
    columns = gateup_part.shape[1]
    g, d = gateup_part.shape[0] // 2, down_part.shape[0] // 2
    gateup = jnp.zeros((count, 2, g, columns), BF)
    down = jnp.zeros((count, 2, d, down_part.shape[1]), BF)
    for step, state in enumerate(states):
        for side in range(2):
            at = (me - step) % count if side == 0 else (me + step) % count
            gateup = lax.dynamic_update_slice(gateup, state[side][None, None, :g], (at, side, 0, 0))
            for n in range(down_part.shape[1] // columns):
                piece = state[side][None, None, g + n * d : g + n * d + d]
                down = lax.dynamic_update_slice(down, piece, (at, side, 0, n * columns))
    return gateup.reshape(-1, columns), down.reshape(-1, down_part.shape[1])


def ring_order(depth, chips):
    if chips != 4:
        return list(range(depth * chips))
    order = []
    for level in range(depth):
        turn = (1, 3, 2) if level % 2 == 0 else (2, 3, 1)
        order += [level * chips + chip for chip in turn]
    return order + [level * chips for level in reversed(range(depth))]


def scatter_sum(term, order):
    devices = [2 * chip + core for chip in order for core in range(2)]
    return lax.psum_scatter(
        term, EVERY, scatter_dimension=0, axis_index_groups=[devices], tiled=True
    )


def in_ring_order(columns, order):
    width = columns.shape[1] // len(order)
    if order == list(range(len(order))):
        return columns
    return jnp.concatenate([columns[:, c * width : (c + 1) * width] for c in order], axis=1)


NT = (((1,), (1,)), ((), ()))
TN = (((0,), (0,)), ((), ()))


def product(left, right, dims=(((1,), (0,)), ((), ()))):
    return lax.dot_general(left, right, dims, preferred_element_type=F32)


def allowed_keys(first_row, rows, span, length):
    row = first_row + lax.broadcasted_iota(jnp.int32, (rows, span), 0)
    key = lax.broadcasted_iota(jnp.int32, (rows, span), 1)
    return (key <= row) & (key < length)


def gathered_kernel(left_ref, weight_ref, out_ref):
    plane, depth, rows, columns = weight_ref.shape
    each = plane * rows
    total = jnp.zeros(out_ref.shape, F32)
    for z in range(depth):
        right = weight_ref[:, z].reshape(each, columns)
        total += product(left_ref[:, z * each : (z + 1) * each], right)
    out_ref[...] = total


def gathered_product(left, weight, columns):
    rows, inner = left.shape
    tile = min(512, columns)
    return pl.pallas_call(
        gathered_kernel,
        grid=(columns // tile,),
        in_specs=[
            pl.BlockSpec((rows, inner), lambda n: (0, 0)),
            pl.BlockSpec(weight.shape[:3] + (tile,), lambda n: (0, 0, 0, n)),
        ],
        out_specs=pl.BlockSpec((rows, tile), lambda n: (0, n)),
        out_shape=jax.ShapeDtypeStruct((rows, columns), F32),
        compiler_params=pltpu.CompilerParams(vmem_limit_bytes=VMEM_BYTES),
        cost_estimate=pl.CostEstimate(
            flops=2 * rows * inner * columns,
            bytes_accessed=2 * inner * columns + 4 * rows * columns,
            transcendentals=0,
        ),
    )(left, weight)


def gathered_back_kernel(left_ref, weight_ref, out_ref):
    plane, _, rows, columns = weight_ref.shape
    right = weight_ref[:, 0].reshape(plane * rows, columns)
    out_ref[...] = product(left_ref[...], right, NT).astype(out_ref.dtype)


def gathered_back(left, weight, dtype):
    rows, columns = left.shape
    plane, depth, each, _ = weight.shape
    return pl.pallas_call(
        gathered_back_kernel,
        grid=(depth,),
        in_specs=[
            pl.BlockSpec((rows, columns), lambda z: (0, 0)),
            pl.BlockSpec((plane, 1, each, columns), lambda z: (0, z, 0, 0)),
        ],
        out_specs=pl.BlockSpec((rows, plane * each), lambda z: (0, z)),
        out_shape=jax.ShapeDtypeStruct((rows, depth * plane * each), dtype),
        compiler_params=pltpu.CompilerParams(vmem_limit_bytes=VMEM_BYTES),
        cost_estimate=pl.CostEstimate(
            flops=2 * rows * columns * depth * plane * each,
            bytes_accessed=2 * columns * (depth * plane * each + rows),
            transcendentals=0,
        ),
    )(left, weight)


def attend_kernel(length_ref, query_ref, key_ref, value_ref, out_ref, total_ref, *, block):
    length = length_ref[0]
    for start in range(0, query_ref.shape[0], block):
        span = start + block
        query = query_ref[start:span, :]
        scores = product(query, key_ref[:span, :], NT) * (HEAD_DIM ** (-0.5))
        allowed = allowed_keys(start, block, span, length)
        scores = jnp.where(allowed, scores, MASK_FILL)
        row_max = jnp.max(scores, axis=1, keepdims=True)
        weights = jnp.where(allowed, jnp.exp(scores - row_max), 0.0)
        row_sum = jnp.sum(weights, axis=1, keepdims=True)
        probs = (weights * (1.0 / row_sum)).astype(BF)
        out_ref[start:span, :] = product(probs, value_ref[:span, :]).astype(BF)
        total_ref[0, start:span, :] = row_max + jnp.log(row_sum)


def attend_back_kernel(
    length_ref,
    query_ref,
    key_ref,
    value_ref,
    back_ref,
    total_ref,
    query_grad_ref,
    key_grad_ref,
    value_grad_ref,
    key_sum,
    value_sum,
    *,
    block,
    group,
):
    length = length_ref[0]
    scale = HEAD_DIM ** (-0.5)
    key_sum[...] = jnp.zeros_like(key_sum)
    value_sum[...] = jnp.zeros_like(value_sum)
    for head in range(group):
        columns = slice(head * HEAD_DIM, (head + 1) * HEAD_DIM)
        for start in range(0, query_ref.shape[0], block):
            span = start + block
            query = query_ref[start:span, columns]
            back = back_ref[start:span, columns]
            key, value = key_ref[:span, :], value_ref[:span, :]
            scores = product(query, key, NT) * scale
            allowed = allowed_keys(start, block, span, length)
            shifted = jnp.where(allowed, scores - total_ref[head, start:span, :], MASK_FILL)
            probs = jnp.exp(shifted)
            prob_back = product(back, value, NT)
            delta = jnp.sum(probs * prob_back, axis=1, keepdims=True)
            score_back = (probs * (prob_back - delta)).astype(BF)
            query_grad_ref[start:span, columns] = (product(score_back, key) * scale).astype(BF)
            key_sum[:span, :] += product(score_back, query, TN)
            value_sum[:span, :] += product(probs.astype(BF), back, TN)
    key_grad_ref[...] = (key_sum[...] * scale).astype(BF)
    value_grad_ref[...] = value_sum[...].astype(BF)


def attend(length, heads, query_each, key_each):
    slots = heads.shape[0]
    group = query_each // key_each
    block = min(256, slots)
    flops = 4 * query_each * slots * slots * HEAD_DIM // 2
    return pl.pallas_call(
        functools.partial(attend_kernel, block=block),
        grid=(query_each,),
        in_specs=[
            pl.BlockSpec(memory_space=pltpu.SMEM),
            pl.BlockSpec((slots, HEAD_DIM), lambda h: (0, h)),
            pl.BlockSpec((slots, HEAD_DIM), lambda h: (0, query_each + h // group)),
            pl.BlockSpec((slots, HEAD_DIM), lambda h: (0, query_each + key_each + h // group)),
        ],
        out_specs=[
            pl.BlockSpec((slots, HEAD_DIM), lambda h: (0, h)),
            pl.BlockSpec((1, slots, 1), lambda h: (h, 0, 0)),
        ],
        out_shape=[
            jax.ShapeDtypeStruct((slots, query_each * HEAD_DIM), BF),
            jax.ShapeDtypeStruct((query_each, slots, 1), F32),
        ],
        compiler_params=pltpu.CompilerParams(vmem_limit_bytes=VMEM_BYTES),
        cost_estimate=pl.CostEstimate(
            flops=flops, bytes_accessed=heads.size * 3, transcendentals=slots * slots
        ),
    )(length, heads, heads, heads)


def attend_back(length, heads, back, total, query_each, key_each):
    slots = heads.shape[0]
    group = query_each // key_each
    block = min(256, slots)
    flops = 10 * query_each * slots * slots * HEAD_DIM // 2
    return pl.pallas_call(
        functools.partial(attend_back_kernel, block=block, group=group),
        grid=(key_each,),
        in_specs=[
            pl.BlockSpec(memory_space=pltpu.SMEM),
            pl.BlockSpec((slots, group * HEAD_DIM), lambda n: (0, n)),
            pl.BlockSpec((slots, HEAD_DIM), lambda n: (0, query_each + n)),
            pl.BlockSpec((slots, HEAD_DIM), lambda n: (0, query_each + key_each + n)),
            pl.BlockSpec((slots, group * HEAD_DIM), lambda n: (0, n)),
            pl.BlockSpec((group, slots, 1), lambda n: (n, 0, 0)),
        ],
        out_specs=[
            pl.BlockSpec((slots, group * HEAD_DIM), lambda n: (0, n)),
            pl.BlockSpec((slots, HEAD_DIM), lambda n: (0, n)),
            pl.BlockSpec((slots, HEAD_DIM), lambda n: (0, n)),
        ],
        out_shape=[
            jax.ShapeDtypeStruct((slots, query_each * HEAD_DIM), BF),
            jax.ShapeDtypeStruct((slots, key_each * HEAD_DIM), BF),
            jax.ShapeDtypeStruct((slots, key_each * HEAD_DIM), BF),
        ],
        scratch_shapes=[pltpu.VMEM((slots, HEAD_DIM), F32), pltpu.VMEM((slots, HEAD_DIM), F32)],
        compiler_params=pltpu.CompilerParams(vmem_limit_bytes=VMEM_BYTES),
        cost_estimate=pl.CostEstimate(
            flops=flops, bytes_accessed=heads.size * 6, transcendentals=slots * slots * 2
        ),
    )(length, heads, heads, heads, back, total)


def feed_kernel(*refs, tiles, units, first, last, names):
    r = dict(zip(names, refs))
    mine = pl.program_id(0) < tiles
    if first:
        second = jnp.where(mine, r["c_own"][...], r["c_oth"][...])
        back = jnp.where(mine, r["d_own"][...], r["d_oth"][...])
        r["c_all"][...] = second
        r["d_all"][...] = back
    else:
        second, back = r["c_in"][...], r["d_in"][...]
    gate_up = product(second, r["gateup"][...])
    gate, up = gate_up[:, :units], gate_up[:, units:]
    sigmoid = 1.0 / (1.0 + jnp.exp(-gate))
    silu = gate * sigmoid
    mixed = (silu * up).astype(BF)
    r["mixed"][...] = mixed
    mixed_back = product(back, r["down"][...], NT)
    gate_back = mixed_back * up * sigmoid * (1.0 + gate * (1.0 - sigmoid))
    both = jnp.concatenate([gate_back, mixed_back * silu], axis=1).astype(BF)
    r["dr"][...] = both
    branch = product(mixed, r["down"][...])
    norm_back = product(both, r["gateup"][...], NT)
    if not first:
        branch = branch + r["o_in"][...].astype(F32)
        norm_back = norm_back + r["n_in"][...].astype(F32)
    branch, norm_back = branch.astype(BF), norm_back.astype(BF)
    if not last:
        r["o_part"][...] = branch
        r["n_part"][...] = norm_back
    else:

        @pl.when(mine)
        def _():
            r["o_own"][...] = branch
            r["n_own"][...] = norm_back

        @pl.when(jnp.logical_not(mine))
        def _():
            r["o_oth"][...] = branch
            r["n_oth"][...] = norm_back


def feed(chunk, block, blocks, gateup, down, tokens, partial, kept):
    first, last = chunk == 0, chunk == CHUNKS - 1
    width, two_units = gateup.shape
    units = two_units // 2
    if first:
        rows = tokens[0].shape[0]
    else:
        rows = partial[0].shape[0] // 2
    tile = min(256, rows)
    tiles = rows // tile
    whole = blocks * 2 * rows
    offset = block * 2 * tiles
    own = pl.BlockSpec((tile, width), lambda t: (jnp.minimum(t, tiles - 1), 0))
    oth = pl.BlockSpec((tile, width), lambda t: (jnp.maximum(t - tiles, 0), 0))
    here = pl.BlockSpec((tile, width), lambda t: (offset + t, 0))
    plain = pl.BlockSpec((tile, width), lambda t: (t, 0))
    once = pl.Buffered(1)
    names, operands, in_specs = [], [], []

    def give(name, value, spec):
        names.append(name)
        operands.append(value)
        in_specs.append(spec)

    if first:
        for name, value, spec in zip(("c_own", "c_oth", "d_own", "d_oth"), tokens, (own, oth) * 2):
            give(name, value, spec)
    else:
        give("c_in", kept["c_all", 0], here)
        give("d_in", kept["d_all", 0], here)
        give("o_in", partial[0], plain)
        give("n_in", partial[1], plain)
    give("gateup", gateup, pl.BlockSpec((width, two_units), lambda t: (0, 0), pipeline_mode=once))
    give("down", down, pl.BlockSpec((units, width), lambda t: (0, 0), pipeline_mode=once))
    outs, out_specs, shapes = [], [], []

    def take(name, shape, spec):
        outs.append(name)
        out_specs.append(spec)
        shapes.append(jax.ShapeDtypeStruct(shape, BF))

    if last:
        for name, spec in zip(("o_own", "o_oth", "n_own", "n_oth"), (own, oth) * 2):
            take(name, (rows, width), spec)
    else:
        take("o_part", (2 * rows, width), plain)
        take("n_part", (2 * rows, width), plain)
    aliases = {}
    held = [("mixed", units), ("dr", two_units)]
    if first:
        held += [("c_all", width), ("d_all", width)]
    for name, columns in held:
        if (name, chunk) in kept:
            aliases[len(operands)] = len(outs)
            give(name + "_kept", kept[name, chunk], pl.BlockSpec(memory_space=pl.ANY))
        take(name, (whole, columns), pl.BlockSpec((tile, columns), lambda t: (offset + t, 0)))
    results = pl.pallas_call(
        functools.partial(
            feed_kernel,
            tiles=tiles,
            units=units,
            first=first,
            last=last,
            names=names + outs,
        ),
        grid=(2 * tiles,),
        in_specs=in_specs,
        out_specs=out_specs,
        out_shape=shapes,
        input_output_aliases=aliases,
        compiler_params=pltpu.CompilerParams(vmem_limit_bytes=VMEM_BYTES),
        cost_estimate=pl.CostEstimate(
            flops=2 * 2 * rows * width * 3 * two_units,
            bytes_accessed=2 * 2 * rows * width * 8,
            transcendentals=2 * rows * units,
        ),
    )(*operands)
    got = dict(zip(outs, results))
    for name, _ in held:
        kept[name, chunk] = got[name]
    return got


def shards(
    hidden,
    cotangent,
    lengths,
    positions,
    query_key_value_master,
    query_key_value_first,
    query_key_value_second,
    out_master,
    out_first,
    out_second,
    gateup_master,
    gateup_first,
    gateup_second,
    down_master,
    down_first,
    down_second,
    gains_master,
    gains_first,
    gains_second,
):
    members, block_length, width = hidden.shape
    depth = lax.axis_size(DEPTH)
    plane = lax.axis_size(PLANE)
    team = lax.axis_size(TEAM)
    team_chips = lax.axis_size("t")
    rows = members * block_length
    length_total = rows * team
    query_width = QUERY_HEADS * HEAD_DIM
    key_width = KEY_VALUE_HEADS * HEAD_DIM
    query_each = QUERY_HEADS // team
    key_each = KEY_VALUE_HEADS // team
    chips = lax.axis_size("p")
    order = ring_order(depth, chips)

    rank = lax.axis_index(DEPTH)
    my_line = lax.axis_index("s")
    member_of_rank = rank % members

    gain_columns = jnp.pad(gains_master.astype(BF).T, ((0, 0), (0, EXTRA - 2)))
    qkv_line = depth_gather(
        jnp.concatenate([query_key_value_master.astype(BF), gain_columns], axis=1)
    )

    def flat_index(line, member):
        return (line * team_chips + member // 2) * 2 + member % 2

    def there_pairs(turn):
        pairs = []
        for r in range(depth):
            for k in range(2):
                i = (r % members + turn) % members
                pairs.append((2 * r + k, flat_index(k * members + i, r // members)))
        return pairs

    def to_sequence(blocks):
        arrived = []
        for turn in range(members):
            sent = pick(blocks, (member_of_rank + turn) % members)
            arrived.append(lax.ppermute(sent, LINE, there_pairs(turn)))
        result = jnp.stack(arrived)
        for turn in range(members):
            result = put(result, arrived[turn], (my_line % members - turn) % members)
        return result.reshape((rows,) + blocks.shape[2:])

    def from_sequence(values):
        blocks = values.reshape((members, block_length) + values.shape[1:])
        arrived = []
        for turn in range(members):
            sent = pick(blocks, (my_line % members - turn) % members)
            back = [(target, source) for source, target in there_pairs(turn)]
            arrived.append(lax.ppermute(sent, LINE, back))
        result = jnp.stack(arrived)
        for turn in range(members):
            result = put(result, arrived[turn], (member_of_rank + turn) % members)
        return result

    slot_ids = rank * block_length + jnp.arange(block_length, dtype=jnp.int32)
    valid = slot_ids[None, :] < lengths[:, None]
    spread = jnp.broadcast_to(lengths[:, None], positions.shape)
    digits = jnp.stack(
        [positions // DIGIT, positions % DIGIT, spread // DIGIT, spread % DIGIT], axis=-1
    ).astype(BF)
    digits = jnp.pad(digits, ((0, 0), (0, 0), (0, EXTRA - 4)))
    ff_block = FF // (depth * plane * CHUNKS)
    gateup_rows = gateup_master.shape[0]
    chunk_width = 2 * depth * ff_block
    gateup_blocks = (
        gateup_master.astype(BF)
        .reshape(gateup_rows, 2, depth, plane, CHUNKS, ff_block)
        .transpose(3, 0, 4, 1, 2, 5)
        .reshape(plane, gateup_rows, CHUNKS * chunk_width)
    )
    hidden_wide = jnp.concatenate([hidden, digits], axis=2)
    qkv_line, gateup_blocks, hidden_wide = tie(qkv_line, gateup_blocks, hidden_wide)
    qkv_ext = lax.all_gather(qkv_line, PLANE, axis=0)
    moved = to_sequence(hidden_wide)
    gateup_mine = exchange(gateup_blocks, PLANE).reshape(plane * gateup_rows, -1)
    masked = jnp.where(valid[..., None], cotangent, jnp.zeros((), BF))
    out_low = out_master.astype(BF)
    moved, gateup_mine, masked, out_low = tie(moved, gateup_mine, masked, out_low)
    out_back_low = to_sequence(masked)
    out_line = depth_gather(out_low)
    down_low = down_master.astype(BF)
    parts = [
        (
            gateup_mine[:, n * chunk_width : (n + 1) * chunk_width],
            down_low[n * ff_block : (n + 1) * ff_block],
        )
        for n in range(CHUNKS)
    ]
    rings = [[pack_weights(*part)] for part in parts]
    turns = [(n, step) for n in range(CHUNKS) for step in range(1, depth)]
    at_once = -(-(depth - 1) // 3)

    def turn_on(count):
        done = []
        for n, _ in turns[: count * at_once]:
            rings[n].append(ring_turn(rings[n][-1]))
            if n not in done:
                done.append(n)
        del turns[: count * at_once]
        return done

    def settle(done, *values):
        flat = []
        for n in done:
            flat += list(rings[n][-1])
        got = tie(*flat, *values)
        for place, n in enumerate(done):
            rings[n][-1] = (got[2 * place], got[2 * place + 1])
        return got[2 * len(done) :]

    first_state = tie(*rings[0][0], out_back_low, out_line)
    rings[0][0] = first_state[:2]
    out_back_low, out_line = first_state[2:]

    numbers = moved[:, width:][:, :4].astype(jnp.int32)
    my_positions = numbers[:, 0] * DIGIT + numbers[:, 1]
    my_length = (numbers[0, 2] * DIGIT + numbers[0, 3]).reshape(1)
    flat_inputs = moved[:, :width].astype(F32)
    all_width = query_width + 2 * key_width
    gains = qkv_ext[..., all_width : all_width + 2].transpose(1, 0, 2, 3).reshape(width, 2)
    gains = gains.astype(F32).T
    first_low = normalize(flat_inputs, gains[0]).astype(BF)
    out_w = lax.all_gather(out_line, PLANE, axis=0)
    projected = gathered_product(first_low, qkv_ext, all_width)
    cosine, sine = rotary_tables(my_positions)
    members_of_team = []
    for u in range(team):
        query = projected[:, u * query_each * HEAD_DIM : (u + 1) * query_each * HEAD_DIM]
        at = query_width + u * key_each * HEAD_DIM
        key = projected[:, at : at + key_each * HEAD_DIM]
        value = projected[:, at + key_width : at + key_width + key_each * HEAD_DIM]
        members_of_team.append(
            jnp.concatenate(
                rotate_heads(query, cosine, sine) + rotate_heads(key, cosine, sine) + [value],
                axis=1,
            ).astype(BF)
        )
    heads = exchange(jnp.stack(members_of_team), TEAM).reshape(length_total, -1)
    half = rows // 2
    relay = chips == 4

    def fan_out(value):
        masks = (1, 2) if relay else range(1, chips)
        return {mask: swap(value, "p", mask) for mask in masks}

    def pass_on(held):
        return [swap(held[1][:half], "p", 2), swap(held[2][half:], "p", 1)]

    dy = fan_out(out_back_low)
    dy_cross = {0: swap(out_back_low, "c", 1)}
    (heads,) = settle(turn_on(1), heads)
    attended_heads, log_total = attend(my_length, heads, query_each, key_each)
    attended_parts = exchange(attended_heads.reshape(team, rows, -1), TEAM)
    keys = sorted(dy)
    got = settle(turn_on(1), attended_parts, dy_cross[0], *[dy[m] for m in keys])
    attended_parts, dy_cross[0] = got[:2]
    dy = dict(zip(keys, got[2:]))
    dy_halves = pass_on(dy) if relay else []
    for mask in keys:
        dy_cross[mask] = swap(dy[mask], "c", 1)
    attended_low = jnp.concatenate([attended_parts[u] for u in range(team)], axis=1)
    middle = flat_inputs + gathered_product(attended_low, out_w, width)
    second_low = normalize(middle, gains[1]).astype(BF)
    flat = [dy_cross[m] for m in keys] + list(dy_halves)
    got = settle(turn_on(1), second_low, *flat)
    second_low = got[0]
    dy_cross.update(zip(keys, got[1:]))
    dy_halves = got[1 + len(keys) :]

    weights = {0: unpack_weights(rings[0], *parts[0])}
    cs = fan_out(second_low)
    cs_cross = {0: swap(second_low, "c", 1)}
    kept = {}
    partials = {}

    def run(chunk, block, tokens):
        got = feed(chunk, block, chips, *weights[chunk], tokens, partials.get(block), kept)
        if chunk < CHUNKS - 1:
            partials[block] = (got["o_part"], got["n_part"])
        return got

    results = {}
    results[0] = run(0, 0, (second_low, cs_cross[0], out_back_low, dy_cross[0]))
    names = [(name, 0) for name in ("mixed", "dr", "c_all", "d_all")]
    if relay:
        dy[3] = jnp.concatenate(dy_halves, axis=0)
        dy_cross[3] = swap(dy[3], "c", 1)
    got = settle(turn_on(1), *[kept[n] for n in names], *[cs[m] for m in keys])
    kept.update(zip(names, got[:4]))
    cs = dict(zip(keys, got[4:]))
    cs_halves = pass_on(cs) if relay else []
    for mask in keys:
        cs_cross[mask] = swap(cs[mask], "c", 1)
    for mask in keys:
        results[mask] = run(0, mask, (cs[mask], cs_cross[mask], dy[mask], dy_cross[mask]))
    got = settle(turn_on(1), *[kept[n] for n in names], *cs_halves)
    kept.update(zip(names, got[:4]))
    if relay:
        cs[3] = jnp.concatenate(got[4:], axis=0)
        cs_cross[3] = swap(cs[3], "c", 1)
        results[3] = run(0, 3, (cs[3], cs_cross[3], dy[3], dy_cross[3]))

    def weight_terms(chunk):
        down_term = jnp.einsum(
            "rc,rk->ck", kept["mixed", chunk], kept["d_all", 0], preferred_element_type=F32
        ).astype(BF)
        gateup_term = jnp.einsum(
            "rc,rk->ck", kept["c_all", 0], kept["dr", chunk], preferred_element_type=F32
        ).astype(BF)
        return down_term, gateup_term

    def packed(terms):
        down_chunks = terms[0].reshape(depth, ff_block, width)
        gateup_chunks = terms[1].reshape(depth, plane * gateup_rows, chunk_width)
        pieces = [
            down_chunks[:, :, at : at + chunk_width] for at in range(0, width, chunk_width)
        ]
        return jnp.concatenate([gateup_chunks] + pieces, axis=1)

    def owners(packed_terms):
        return lax.psum_scatter(packed_terms, DEPTH, scatter_dimension=0)

    terms = weight_terms(0)
    got = settle(turn_on(len(turns)), packed(terms), kept["c_all", 0], kept["d_all", 0])
    kept["c_all", 0], kept["d_all", 0] = got[1:]
    sums = {0: owners(got[0])}
    for chunk in range(1, CHUNKS):
        weights[chunk] = unpack_weights(rings[chunk], *parts[chunk])

    def chip_sum(own, other):
        return (own.astype(F32) + swap(other, "c", 1).astype(F32)).astype(BF)

    norm_sums = {}
    block_order = (3, 1, 2, 0) if relay else (*range(1, chips), 0)
    for chunk in range(1, CHUNKS):
        waiting = None
        for mask in block_order:
            results[mask] = run(chunk, mask, None)
            if chunk < CHUNKS - 1:
                continue
            arriving = swap(results[mask]["n_oth"], "c", 1)
            if waiting is not None:
                before, arrived = waiting
                kept["dr", chunk], arrived = tie(kept["dr", chunk], arrived)
                norm_sums[before] = total_of([results[before]["n_own"], arrived]).astype(BF)
                norm_sums[before] = swap(norm_sums[before], "p", before)
            waiting = mask, arriving
        if chunk == CHUNKS - 1:
            norm_sums[0] = total_of([results[0]["n_own"], waiting[1]]).astype(BF)
    last = CHUNKS - 1
    terms = weight_terms(last)
    branch_own = [results[mask]["o_own"] for mask in range(chips)]
    branch_oth = [results[mask]["o_oth"] for mask in range(chips)]
    sums[0], last_terms, *got = tie(
        sums[0],
        packed(terms),
        *[norm_sums[mask] for mask in range(chips)],
        *branch_own,
        *branch_oth,
    )
    norm_back = total_of(got[:chips])
    sums[last] = owners(last_terms)
    branch_own, branch_oth = got[chips : 2 * chips], got[2 * chips :]
    branch = [chip_sum(branch_own[0], branch_oth[0])]
    for mask in range(1, chips):
        branch.append(swap(chip_sum(branch_own[mask], branch_oth[mask]), "p", mask))

    _, second_pull = jax.vjp(normalize, middle, gains[1])
    middle_norm_back, second_gain_grad = second_pull(norm_back)
    middle_back = out_back_low.astype(F32) + middle_norm_back
    branch_low = middle_back.astype(BF)

    attended_back = gathered_back(branch_low, out_w, BF)
    group_width = query_each * HEAD_DIM
    back_blocks = jnp.stack(
        [attended_back[:, u * group_width : (u + 1) * group_width] for u in range(team)]
    )
    back_rows = exchange(back_blocks, TEAM).reshape(length_total, group_width)
    out_term = jnp.einsum(
        "rc,rk->ck", in_ring_order(attended_low, order), branch_low, preferred_element_type=F32
    ).astype(BF)
    out_grad = scatter_sum(out_term, order)
    head_grads = attend_back(my_length, heads, back_rows, log_total, query_each, key_each)
    query_back, key_back, value_back = [
        exchange(grad.reshape(team, rows, -1), TEAM) for grad in head_grads
    ]
    columns = []
    for back in (query_back, key_back):
        for u in range(team):
            columns += rotate_heads(back[u].astype(F32), cosine, -sine)
    columns = [part.astype(BF) for part in columns] + [value_back[u] for u in range(team)]
    projected_back = jnp.concatenate(columns, axis=1)
    first_back = gathered_back(projected_back, qkv_ext, F32)
    _, first_pull = jax.vjp(normalize, flat_inputs, gains[0])
    input_norm_back, first_gain_grad = first_pull(first_back)
    input_back = from_sequence((middle_back + input_norm_back).astype(BF))

    qkv_term = jnp.einsum(
        "rc,rk->ck", in_ring_order(first_low, order), projected_back, preferred_element_type=F32
    ).astype(BF)
    gain_terms = jnp.stack([first_gain_grad, second_gain_grad]).astype(BF)
    gain_terms = jnp.pad(in_ring_order(gain_terms, order).T, ((0, 0), (0, EXTRA - 2)))
    grown = plane * gateup_rows
    gateup_sum = jnp.concatenate([sums[n][:grown] for n in range(CHUNKS)], axis=1)
    down_grad = jnp.concatenate(
        [
            jnp.concatenate(
                [
                    sums[n][at : at + ff_block].astype(F32)
                    for at in range(grown, sums[n].shape[0], ff_block)
                ],
                axis=1,
            )
            for n in range(CHUNKS)
        ],
        axis=0,
    )
    qkv_term, *branch = tie(qkv_term, *branch)
    output = from_sequence((middle + total_of(branch)).astype(BF))
    gateup_grad = (
        exchange(gateup_sum.reshape(plane, gateup_rows, CHUNKS * chunk_width), PLANE)
        .reshape(plane, gateup_rows, CHUNKS, 2, depth, ff_block)
        .transpose(1, 3, 4, 0, 2, 5)
        .reshape(gateup_rows, 2 * FF)
    )
    qkv_sum = scatter_sum(jnp.concatenate([qkv_term, gain_terms], axis=1), order)
    qkv_grad = qkv_sum[:, :all_width].astype(F32)
    gains_grad = qkv_sum[:, all_width : all_width + 2].astype(F32).T

    qkv_set = adamw_update(
        query_key_value_master,
        query_key_value_first,
        query_key_value_second,
        qkv_grad,
        MODEL_DIM ** (-0.5),
    )
    out_set = adamw_update(out_master, out_first, out_second, out_grad.astype(F32), OUT_RATE)
    gateup_set = adamw_update(
        gateup_master,
        gateup_first,
        gateup_second,
        gateup_grad.astype(F32),
        MODEL_DIM ** (-0.5),
    )
    down_set = adamw_update(
        down_master, down_first, down_second, down_grad, FF ** (-0.5)
    )
    gains_set = adamw_update(gains_master, gains_first, gains_second, gains_grad, GAIN_RATE)
    return (
        (output, input_back) + qkv_set + out_set + gateup_set + down_set + gains_set
    )


def solution(mesh):
    ctx, fsdp = mesh.shape["ctx"], mesh.shape["fsdp"]
    line_count = 4
    fine = Mesh(mesh.devices.reshape(line_count, ctx // line_count, fsdp // 2, 2), EVERY)
    tokens = P(PLANE, DEPTH, None)
    weight = P(EVERY, None)
    gain = P(None, EVERY)
    return jax.shard_map(
        shards,
        mesh=fine,
        in_specs=(tokens, tokens, P(PLANE), P(PLANE, DEPTH)) + (weight,) * 12 + (gain,) * 3,
        out_specs=(tokens, tokens) + (weight,) * 16 + (gain,) * 4,
        check_vma=False,
    )
```

```python
import functools

import jax
import jax.numpy as jnp
from jax import lax
from jax.experimental import pallas as pl
from jax.experimental.pallas import tpu as pltpu
from jax.sharding import Mesh
from jax.sharding import PartitionSpec as P

MODEL_DIM = 2048
QUERY_HEADS = 8
KEY_VALUE_HEADS = 4
HEAD_DIM = 256
FF = 8192
STEP = 10

NORM_EPS = 1e-06
ROPE_BASE = 1000042.0
BETA_ONE = 0.5
BETA_TWO = 0.5
ADAM_EPS = 1e-08
DECAY_RATE = 0.1
GAIN_RATE = 0.3
OUT_RATE = 0.25
MASK_FILL = -1e30

EVERY = ("s", "t", "p", "c")
DEPTH = ("s", "t")
PLANE = ("p", "c")
TEAM = ("t", "c")
LINE = ("s", "t", "c")
EXTRA = 128
DIGIT = 64
CHUNKS = 2
VMEM_BYTES = 52 * 1024 * 1024

BF = jnp.bfloat16
F32 = jnp.float32


def normalize(values, gain):
    return values * lax.rsqrt(jnp.mean(values * values, axis=-1, keepdims=True) + NORM_EPS) * gain


def rotary_tables(seq_positions):
    half_width = HEAD_DIM // 2
    inverse_freq = jnp.exp(
        -jnp.log(ROPE_BASE) * (jnp.arange(half_width, dtype=F32) * 2.0 / HEAD_DIM)
    )
    angles = seq_positions.astype(F32)[..., None] * inverse_freq
    return jnp.cos(angles), jnp.sin(angles)


def adamw_update(master, first_moment, second_moment, gradient, step_rate):
    first_new = BETA_ONE * first_moment + (1.0 - BETA_ONE) * gradient
    second_new = BETA_TWO * second_moment + (1.0 - BETA_TWO) * gradient * gradient
    first_hat = first_new / (1.0 - BETA_ONE**STEP)
    second_hat = second_new / (1.0 - BETA_TWO**STEP)
    master_new = master - step_rate * (
        first_hat / (jnp.sqrt(second_hat) + ADAM_EPS) + DECAY_RATE * master
    )
    return (master_new, first_new, second_new, master_new.astype(BF))


def tie(*values):
    return lax.optimization_barrier(values)


def pick(blocks, index, axis=0):
    return lax.dynamic_index_in_dim(blocks, index, axis, keepdims=False)


def put(buffer, block, index):
    return lax.dynamic_update_index_in_dim(buffer, block, index, 0)


def swap(value, axes, mask):
    count = lax.axis_size(axes)
    return lax.ppermute(value, axes, [(source, source ^ mask) for source in range(count)])


def exchange(blocks, axes):
    me = lax.axis_index(axes)
    result = blocks
    for mask in range(1, blocks.shape[0]):
        result = put(result, swap(pick(blocks, me ^ mask), axes, mask), me ^ mask)
    return result


def total_of(terms):
    total = terms[0].astype(F32)
    for term in terms[1:]:
        total = total + term.astype(F32)
    return total


def depth_gather(block):
    me = lax.axis_index(DEPTH)
    count = lax.axis_size(DEPTH)
    result = put(jnp.zeros((count,) + block.shape, block.dtype), block, me)
    for mask in range(1, count):
        result = put(result, swap(block, DEPTH, mask), me ^ mask)
    return result


def halving_stages(count):
    return [1 << bit for bit in range(count.bit_length() - 1)]


def toward(blocks, axes):
    me = lax.axis_index(axes)
    return jnp.stack([pick(blocks, me ^ mask) for mask in range(blocks.shape[0])])


def halve(blocks, axes, bit):
    count = blocks.shape[0]
    pairs = blocks.reshape((count // (2 * bit), 2, bit) + blocks.shape[1:])
    moved = swap(pairs[:, 1], axes, bit)
    return jnp.stack([pairs[:, 0], moved], axis=1).reshape(blocks.shape)


def in_place(blocks, axes):
    me = lax.axis_index(axes)
    return jnp.stack([pick(blocks, me ^ index) for index in range(blocks.shape[0])])


def ring_turn(state):
    ahead, behind = state
    count = lax.axis_size(DEPTH)
    up = [(source, (source + 1) % count) for source in range(count)]
    down = [(source, (source - 1) % count) for source in range(count)]
    return lax.ppermute(ahead, DEPTH, up), lax.ppermute(behind, DEPTH, down)


def pack_weights(gateup_part, down_part):
    columns = gateup_part.shape[1]
    halves = []
    for side in range(2):
        g, d = gateup_part.shape[0] // 2, down_part.shape[0] // 2
        rows = down_part[side * d : side * d + d]
        pieces = [rows[:, at : at + columns] for at in range(0, rows.shape[1], columns)]
        halves.append(
            jnp.concatenate([gateup_part[side * g : side * g + g]] + pieces, axis=0)
        )
    return tuple(halves)


def unpack_weights(states, gateup_part, down_part):
    count = lax.axis_size(DEPTH)
    me = lax.axis_index(DEPTH)
    columns = gateup_part.shape[1]
    g, d = gateup_part.shape[0] // 2, down_part.shape[0] // 2
    gateup = jnp.zeros((count, 2, g, columns), BF)
    down = jnp.zeros((count, 2, d, down_part.shape[1]), BF)
    for step, state in enumerate(states):
        for side in range(2):
            at = (me - step) % count if side == 0 else (me + step) % count
            gateup = lax.dynamic_update_slice(gateup, state[side][None, None, :g], (at, side, 0, 0))
            for n in range(down_part.shape[1] // columns):
                piece = state[side][None, None, g + n * d : g + n * d + d]
                down = lax.dynamic_update_slice(down, piece, (at, side, 0, n * columns))
    return gateup.reshape(-1, columns), down.reshape(-1, down_part.shape[1])


def ring_order(depth, chips):
    if chips != 4:
        return list(range(depth * chips))
    order = []
    for level in range(depth):
        turn = (1, 3, 2) if level % 2 == 0 else (2, 3, 1)
        order += [level * chips + chip for chip in turn]
    return order + [level * chips for level in reversed(range(depth))]


def scatter_sum(term, order):
    devices = [2 * chip + core for chip in order for core in range(2)]
    return lax.psum_scatter(
        term, EVERY, scatter_dimension=0, axis_index_groups=[devices], tiled=True
    )


def in_ring_order(columns, order):
    rows = columns.T
    if order == list(range(len(order))):
        return rows
    each = rows.shape[0] // len(order)
    return jnp.concatenate([rows[c * each : (c + 1) * each] for c in order], axis=0)


NT = (((1,), (1,)), ((), ()))
TN = (((0,), (0,)), ((), ()))


def product(left, right, dims=(((1,), (0,)), ((), ()))):
    return lax.dot_general(left, right, dims, preferred_element_type=F32)


def allowed_keys(first_row, rows, span, length):
    row = first_row + lax.broadcasted_iota(jnp.int32, (rows, span), 0)
    key = lax.broadcasted_iota(jnp.int32, (rows, span), 1)
    return (key <= row) & (key < length)


def gathered_kernel(left_ref, weight_ref, out_ref):
    plane, depth, rows, columns = weight_ref.shape
    each = plane * rows
    total = jnp.zeros(out_ref.shape, F32)
    for z in range(depth):
        right = weight_ref[:, z].reshape(each, columns)
        total += product(left_ref[:, z * each : (z + 1) * each], right)
    out_ref[...] = total


def gathered_product(left, weight, columns):
    rows, inner = left.shape
    tile = min(512, columns)
    return pl.pallas_call(
        gathered_kernel,
        grid=(columns // tile,),
        in_specs=[
            pl.BlockSpec((rows, inner), lambda n: (0, 0)),
            pl.BlockSpec(weight.shape[:3] + (tile,), lambda n: (0, 0, 0, n)),
        ],
        out_specs=pl.BlockSpec((rows, tile), lambda n: (0, n)),
        out_shape=jax.ShapeDtypeStruct((rows, columns), F32),
        compiler_params=pltpu.CompilerParams(vmem_limit_bytes=VMEM_BYTES),
        cost_estimate=pl.CostEstimate(
            flops=2 * rows * inner * columns,
            bytes_accessed=2 * inner * columns + 4 * rows * columns,
            transcendentals=0,
        ),
    )(left, weight)


def rotated(columns, cosine, sine):
    half = HEAD_DIM // 2
    first, second = columns[:, :half], columns[:, half:]
    return jnp.concatenate(
        [first * cosine - second * sine, second * cosine + first * sine], axis=1
    )


def project_kernel(left_ref, weight_ref, cosine_ref, sine_ref, out_ref):
    plane, depth, rows, columns = weight_ref.shape
    each = plane * rows
    total = jnp.zeros((left_ref.shape[0], columns), F32)
    for z in range(depth):
        right = weight_ref[:, z].reshape(each, columns)
        total += product(left_ref[:, z * each : (z + 1) * each], right)
    turns = pl.program_id(0) < QUERY_HEADS + KEY_VALUE_HEADS

    @pl.when(turns)
    def _():
        out_ref[0] = rotated(total, cosine_ref[...], sine_ref[...]).astype(BF)

    @pl.when(jnp.logical_not(turns))
    def _():
        out_ref[0] = total.astype(BF)


def head_place(n, team):
    query_each, key_each = QUERY_HEADS // team, KEY_VALUE_HEADS // team
    key = n - QUERY_HEADS
    value = key - KEY_VALUE_HEADS
    is_query, is_key = n < QUERY_HEADS, key < KEY_VALUE_HEADS
    member = jnp.where(
        is_query, n // query_each, jnp.where(is_key, key // key_each, value // key_each)
    )
    place = jnp.where(
        is_query,
        n % query_each,
        query_each + jnp.where(is_key, key % key_each, key_each + value % key_each),
    )
    return member, place


def project(left, weight, cosine, sine, team):
    rows, inner = left.shape
    heads = QUERY_HEADS + 2 * KEY_VALUE_HEADS
    half = HEAD_DIM // 2

    def place(n):
        member, column = head_place(n, team)
        return (member, 0, column)

    return pl.pallas_call(
        project_kernel,
        grid=(heads,),
        in_specs=[
            pl.BlockSpec((rows, inner), lambda n: (0, 0)),
            pl.BlockSpec(weight.shape[:3] + (HEAD_DIM,), lambda n: (0, 0, 0, n)),
            pl.BlockSpec((rows, half), lambda n: (0, 0)),
            pl.BlockSpec((rows, half), lambda n: (0, 0)),
        ],
        out_specs=pl.BlockSpec((1, rows, HEAD_DIM), place),
        out_shape=jax.ShapeDtypeStruct((team, rows, heads // team * HEAD_DIM), BF),
        compiler_params=pltpu.CompilerParams(vmem_limit_bytes=VMEM_BYTES),
        cost_estimate=pl.CostEstimate(
            flops=2 * rows * inner * heads * HEAD_DIM,
            bytes_accessed=2 * heads * HEAD_DIM * (inner + rows),
            transcendentals=0,
        ),
    )(left, weight, cosine, sine)


def unturn_kernel(query_ref, key_ref, value_ref, cosine_ref, sine_ref, out_ref):
    n = pl.program_id(0)
    cosine, sine = cosine_ref[...], sine_ref[...]

    @pl.when(n < QUERY_HEADS)
    def _():
        out_ref[...] = rotated(query_ref[0].astype(F32), cosine, -sine).astype(BF)

    @pl.when(jnp.logical_and(n >= QUERY_HEADS, n < QUERY_HEADS + KEY_VALUE_HEADS))
    def _():
        out_ref[...] = rotated(key_ref[0].astype(F32), cosine, -sine).astype(BF)

    @pl.when(n >= QUERY_HEADS + KEY_VALUE_HEADS)
    def _():
        out_ref[...] = value_ref[0]


def unturn(query, key, value, cosine, sine):
    team, rows, _ = query.shape
    heads = QUERY_HEADS + 2 * KEY_VALUE_HEADS
    half = HEAD_DIM // 2

    def spec(first, count):
        each = count // team

        def place(n):
            head = jnp.clip(n - first, 0, count - 1)
            return (head // each, 0, head % each)

        return pl.BlockSpec((1, rows, HEAD_DIM), place)

    table = pl.BlockSpec((rows, half), lambda n: (0, 0))
    return pl.pallas_call(
        unturn_kernel,
        grid=(heads,),
        in_specs=[
            spec(0, QUERY_HEADS),
            spec(QUERY_HEADS, KEY_VALUE_HEADS),
            spec(QUERY_HEADS + KEY_VALUE_HEADS, KEY_VALUE_HEADS),
            table,
            table,
        ],
        out_specs=pl.BlockSpec((rows, HEAD_DIM), lambda n: (0, n)),
        out_shape=jax.ShapeDtypeStruct((rows, heads * HEAD_DIM), BF),
        compiler_params=pltpu.CompilerParams(vmem_limit_bytes=VMEM_BYTES),
        cost_estimate=pl.CostEstimate(
            flops=4 * rows * heads * HEAD_DIM,
            bytes_accessed=4 * rows * heads * HEAD_DIM,
            transcendentals=0,
        ),
    )(query, key, value, cosine, sine)


def terms_kernel(first_ref, out_ref, first_right_ref, out_right_ref, gain_ref, result_ref, *, at):
    n = pl.program_id(0)

    @pl.when(n < at[0])
    def _():
        result_ref[...] = product(first_ref[...], first_right_ref[...]).astype(BF)

    @pl.when(jnp.logical_and(n >= at[0], n < at[1]))
    def _():
        result_ref[...] = product(out_ref[...], out_right_ref[...]).astype(BF)

    @pl.when(n >= at[1])
    def _():
        result_ref[:, : gain_ref.shape[1]] = gain_ref[...]


def gradient_terms(first, first_right, out, out_right, gain):
    inner, rows = first.shape
    tile = min(512, out_right.shape[1])
    counts = [first_right.shape[1] // tile, out_right.shape[1] // tile]
    at = (counts[0], counts[0] + counts[1])
    total = first_right.shape[1] + out_right.shape[1] + gain.shape[1]
    whole = pl.BlockSpec((inner, rows), lambda n: (0, 0))
    return pl.pallas_call(
        functools.partial(terms_kernel, at=at),
        grid=(at[1] + 1,),
        in_specs=[
            whole,
            whole,
            pl.BlockSpec((rows, tile), lambda n: (0, jnp.clip(n, 0, counts[0] - 1))),
            pl.BlockSpec((rows, tile), lambda n: (0, jnp.clip(n - at[0], 0, counts[1] - 1))),
            pl.BlockSpec(gain.shape, lambda n: (0, 0)),
        ],
        out_specs=pl.BlockSpec((inner, tile), lambda n: (0, n)),
        out_shape=jax.ShapeDtypeStruct((inner, total), BF),
        compiler_params=pltpu.CompilerParams(vmem_limit_bytes=VMEM_BYTES),
        cost_estimate=pl.CostEstimate(
            flops=2 * rows * inner * total, bytes_accessed=4 * inner * total, transcendentals=0
        ),
    )(first, out, first_right, out_right, gain)


def gathered_back_kernel(left_ref, weight_ref, out_ref):
    plane, _, rows, columns = weight_ref.shape
    right = weight_ref[:, 0].reshape(plane * rows, columns)
    out_ref[...] = product(left_ref[...], right, NT).astype(out_ref.dtype)


def gathered_back(left, weight, dtype):
    rows, columns = left.shape
    plane, depth, each, _ = weight.shape
    return pl.pallas_call(
        gathered_back_kernel,
        grid=(depth,),
        in_specs=[
            pl.BlockSpec((rows, columns), lambda z: (0, 0)),
            pl.BlockSpec((plane, 1, each, columns), lambda z: (0, z, 0, 0)),
        ],
        out_specs=pl.BlockSpec((rows, plane * each), lambda z: (0, z)),
        out_shape=jax.ShapeDtypeStruct((rows, depth * plane * each), dtype),
        compiler_params=pltpu.CompilerParams(vmem_limit_bytes=VMEM_BYTES),
        cost_estimate=pl.CostEstimate(
            flops=2 * rows * columns * depth * plane * each,
            bytes_accessed=2 * columns * (depth * plane * each + rows),
            transcendentals=0,
        ),
    )(left, weight)


def attend_kernel(length_ref, query_ref, key_ref, value_ref, out_ref, total_ref, *, block):
    length = length_ref[0]
    for start in range(0, query_ref.shape[0], block):
        span = start + block
        query = query_ref[start:span, :]
        scores = product(query, key_ref[:span, :], NT) * (HEAD_DIM ** (-0.5))
        allowed = allowed_keys(start, block, span, length)
        scores = jnp.where(allowed, scores, MASK_FILL)
        row_max = jnp.max(scores, axis=1, keepdims=True)
        weights = jnp.where(allowed, jnp.exp(scores - row_max), 0.0)
        row_sum = jnp.sum(weights, axis=1, keepdims=True)
        probs = (weights * (1.0 / row_sum)).astype(BF)
        out_ref[start:span, :] = product(probs, value_ref[:span, :]).astype(BF)
        total_ref[0, start:span, :] = row_max + jnp.log(row_sum)


def attend_back_kernel(
    length_ref,
    query_ref,
    key_ref,
    value_ref,
    back_ref,
    total_ref,
    query_grad_ref,
    key_grad_ref,
    value_grad_ref,
    key_sum,
    value_sum,
    *,
    block,
    group,
):
    length = length_ref[0]
    scale = HEAD_DIM ** (-0.5)
    key_sum[...] = jnp.zeros_like(key_sum)
    value_sum[...] = jnp.zeros_like(value_sum)
    for head in range(group):
        columns = slice(head * HEAD_DIM, (head + 1) * HEAD_DIM)
        for start in range(0, query_ref.shape[0], block):
            span = start + block
            query = query_ref[start:span, columns]
            back = back_ref[start:span, columns]
            key, value = key_ref[:span, :], value_ref[:span, :]
            scores = product(query, key, NT) * scale
            allowed = allowed_keys(start, block, span, length)
            shifted = jnp.where(allowed, scores - total_ref[head, start:span, :], MASK_FILL)
            probs = jnp.exp(shifted)
            prob_back = product(back, value, NT)
            delta = jnp.sum(probs * prob_back, axis=1, keepdims=True)
            score_back = (probs * (prob_back - delta)).astype(BF)
            query_grad_ref[start:span, columns] = (product(score_back, key) * scale).astype(BF)
            key_sum[:span, :] += product(score_back, query, TN)
            value_sum[:span, :] += product(probs.astype(BF), back, TN)
    key_grad_ref[...] = (key_sum[...] * scale).astype(BF)
    value_grad_ref[...] = value_sum[...].astype(BF)


def attend(length, heads, query_each, key_each):
    slots = heads.shape[0]
    group = query_each // key_each
    block = min(256, slots)
    flops = 4 * query_each * slots * slots * HEAD_DIM // 2
    return pl.pallas_call(
        functools.partial(attend_kernel, block=block),
        grid=(query_each,),
        in_specs=[
            pl.BlockSpec(memory_space=pltpu.SMEM),
            pl.BlockSpec((slots, HEAD_DIM), lambda h: (0, h)),
            pl.BlockSpec((slots, HEAD_DIM), lambda h: (0, query_each + h // group)),
            pl.BlockSpec((slots, HEAD_DIM), lambda h: (0, query_each + key_each + h // group)),
        ],
        out_specs=[
            pl.BlockSpec((slots, HEAD_DIM), lambda h: (0, h)),
            pl.BlockSpec((1, slots, 1), lambda h: (h, 0, 0)),
        ],
        out_shape=[
            jax.ShapeDtypeStruct((slots, query_each * HEAD_DIM), BF),
            jax.ShapeDtypeStruct((query_each, slots, 1), F32),
        ],
        compiler_params=pltpu.CompilerParams(vmem_limit_bytes=VMEM_BYTES),
        cost_estimate=pl.CostEstimate(
            flops=flops, bytes_accessed=heads.size * 3, transcendentals=slots * slots
        ),
    )(length, heads, heads, heads)


def attend_back(length, heads, back, total, query_each, key_each):
    slots = heads.shape[0]
    group = query_each // key_each
    block = min(256, slots)
    flops = 10 * query_each * slots * slots * HEAD_DIM // 2
    return pl.pallas_call(
        functools.partial(attend_back_kernel, block=block, group=group),
        grid=(key_each,),
        in_specs=[
            pl.BlockSpec(memory_space=pltpu.SMEM),
            pl.BlockSpec((slots, group * HEAD_DIM), lambda n: (0, n)),
            pl.BlockSpec((slots, HEAD_DIM), lambda n: (0, query_each + n)),
            pl.BlockSpec((slots, HEAD_DIM), lambda n: (0, query_each + key_each + n)),
            pl.BlockSpec((slots, group * HEAD_DIM), lambda n: (0, n)),
            pl.BlockSpec((group, slots, 1), lambda n: (n, 0, 0)),
        ],
        out_specs=[
            pl.BlockSpec((slots, group * HEAD_DIM), lambda n: (0, n)),
            pl.BlockSpec((slots, HEAD_DIM), lambda n: (0, n)),
            pl.BlockSpec((slots, HEAD_DIM), lambda n: (0, n)),
        ],
        out_shape=[
            jax.ShapeDtypeStruct((slots, query_each * HEAD_DIM), BF),
            jax.ShapeDtypeStruct((slots, key_each * HEAD_DIM), BF),
            jax.ShapeDtypeStruct((slots, key_each * HEAD_DIM), BF),
        ],
        scratch_shapes=[pltpu.VMEM((slots, HEAD_DIM), F32), pltpu.VMEM((slots, HEAD_DIM), F32)],
        compiler_params=pltpu.CompilerParams(vmem_limit_bytes=VMEM_BYTES),
        cost_estimate=pl.CostEstimate(
            flops=flops, bytes_accessed=heads.size * 6, transcendentals=slots * slots * 2
        ),
    )(length, heads, heads, heads, back, total)


def feed_kernel(*refs, tiles, units, first, last, names):
    r = dict(zip(names, refs))
    mine = pl.program_id(0) < tiles
    if first:
        second = jnp.where(mine, r["c_own"][...], r["c_oth"][...])
        back = jnp.where(mine, r["d_own"][...], r["d_oth"][...])
        r["c_all"][...] = second
        r["d_all"][...] = back
    else:
        second, back = r["c_in"][...], r["d_in"][...]
    gate_up = product(second, r["gateup"][...])
    gate, up = gate_up[:, :units], gate_up[:, units:]
    sigmoid = 1.0 / (1.0 + jnp.exp(-gate))
    silu = gate * sigmoid
    mixed = (silu * up).astype(BF)
    r["mixed"][...] = mixed
    mixed_back = product(back, r["down"][...], NT)
    gate_back = mixed_back * up * sigmoid * (1.0 + gate * (1.0 - sigmoid))
    both = jnp.concatenate([gate_back, mixed_back * silu], axis=1).astype(BF)
    r["dr"][...] = both
    branch = product(mixed, r["down"][...])
    norm_back = product(both, r["gateup"][...], NT)
    if not first:
        branch = branch + r["o_in"][...].astype(F32)
        norm_back = norm_back + r["n_in"][...].astype(F32)
    branch, norm_back = branch.astype(BF), norm_back.astype(BF)
    if not last:
        r["o_part"][...] = branch
        r["n_part"][...] = norm_back
    else:

        @pl.when(mine)
        def _():
            r["o_own"][...] = branch
            r["n_own"][...] = norm_back

        @pl.when(jnp.logical_not(mine))
        def _():
            r["o_oth"][...] = branch
            r["n_oth"][...] = norm_back


def feed(chunk, block, blocks, gateup, down, tokens, partial, kept):
    first, last = chunk == 0, chunk == CHUNKS - 1
    width, two_units = gateup.shape
    units = two_units // 2
    if first:
        rows = tokens[0].shape[-2]
    else:
        rows = partial[0].shape[0] // 2
    tile = min(256, rows)
    tiles = rows // tile
    whole = blocks * 2 * rows
    offset = block * 2 * tiles
    own = pl.BlockSpec((tile, width), lambda t: (jnp.minimum(t, tiles - 1), 0))
    oth = pl.BlockSpec((tile, width), lambda t: (jnp.maximum(t - tiles, 0), 0))
    here = pl.BlockSpec((tile, width), lambda t: (offset + t, 0))
    plain = pl.BlockSpec((tile, width), lambda t: (t, 0))
    once = pl.Buffered(1)
    names, operands, in_specs = [], [], []

    def give(name, value, spec):
        names.append(name)
        operands.append(value)
        in_specs.append(spec)

    if first:
        pieces = zip(("c_own", "c_oth", "d_own", "d_oth"), tokens, (own, oth) * 2, (0, 0, 1, 1))
        for name, value, spec, lead in pieces:
            if value.ndim == 3:
                spec = pl.BlockSpec(
                    (None, tile, width),
                    lambda t, lead=lead, place=spec.index_map: (lead,) + place(t),
                )
            give(name, value, spec)
    else:
        give("c_in", kept["c_all", 0], here)
        give("d_in", kept["d_all", 0], here)
        give("o_in", partial[0], plain)
        give("n_in", partial[1], plain)
    give("gateup", gateup, pl.BlockSpec((width, two_units), lambda t: (0, 0), pipeline_mode=once))
    give("down", down, pl.BlockSpec((units, width), lambda t: (0, 0), pipeline_mode=once))
    outs, out_specs, shapes = [], [], []

    def take(name, shape, spec):
        outs.append(name)
        out_specs.append(spec)
        shapes.append(jax.ShapeDtypeStruct(shape, BF))

    if last:
        for name, spec in zip(("o_own", "o_oth", "n_own", "n_oth"), (own, oth) * 2):
            take(name, (rows, width), spec)
    else:
        take("o_part", (2 * rows, width), plain)
        take("n_part", (2 * rows, width), plain)
    aliases = {}
    held = [("mixed", units), ("dr", two_units)]
    if first:
        held += [("c_all", width), ("d_all", width)]
    for name, columns in held:
        if (name, chunk) in kept:
            aliases[len(operands)] = len(outs)
            give(name + "_kept", kept[name, chunk], pl.BlockSpec(memory_space=pl.ANY))
        take(name, (whole, columns), pl.BlockSpec((tile, columns), lambda t: (offset + t, 0)))
    results = pl.pallas_call(
        functools.partial(
            feed_kernel,
            tiles=tiles,
            units=units,
            first=first,
            last=last,
            names=names + outs,
        ),
        grid=(2 * tiles,),
        in_specs=in_specs,
        out_specs=out_specs,
        out_shape=shapes,
        input_output_aliases=aliases,
        compiler_params=pltpu.CompilerParams(vmem_limit_bytes=VMEM_BYTES),
        cost_estimate=pl.CostEstimate(
            flops=2 * 2 * rows * width * 3 * two_units,
            bytes_accessed=2 * 2 * rows * width * 8,
            transcendentals=2 * rows * units,
        ),
    )(*operands)
    got = dict(zip(outs, results))
    for name, _ in held:
        kept[name, chunk] = got[name]
    return got


def shards(
    hidden,
    cotangent,
    lengths,
    positions,
    query_key_value_master,
    query_key_value_first,
    query_key_value_second,
    out_master,
    out_first,
    out_second,
    gateup_master,
    gateup_first,
    gateup_second,
    down_master,
    down_first,
    down_second,
    gains_master,
    gains_first,
    gains_second,
):
    members, block_length, width = hidden.shape
    depth = lax.axis_size(DEPTH)
    plane = lax.axis_size(PLANE)
    team = lax.axis_size(TEAM)
    team_chips = lax.axis_size("t")
    rows = members * block_length
    length_total = rows * team
    query_width = QUERY_HEADS * HEAD_DIM
    key_width = KEY_VALUE_HEADS * HEAD_DIM
    query_each = QUERY_HEADS // team
    key_each = KEY_VALUE_HEADS // team
    chips = lax.axis_size("p")
    order = ring_order(depth, chips)

    rank = lax.axis_index(DEPTH)
    my_line = lax.axis_index("s")
    member_of_rank = rank % members

    gain_columns = jnp.pad(gains_master.astype(BF).T, ((0, 0), (0, EXTRA - 2)))
    qkv_line = depth_gather(
        jnp.concatenate([query_key_value_master.astype(BF), gain_columns], axis=1)
    )

    def flat_index(line, member):
        return (line * team_chips + member // 2) * 2 + member % 2

    def there_pairs(turn):
        pairs = []
        for r in range(depth):
            for k in range(2):
                i = (r % members + turn) % members
                pairs.append((2 * r + k, flat_index(k * members + i, r // members)))
        return pairs

    def to_sequence(blocks):
        arrived = []
        for turn in range(members):
            sent = pick(blocks, (member_of_rank + turn) % members)
            arrived.append(lax.ppermute(sent, LINE, there_pairs(turn)))
        result = jnp.stack(arrived)
        for turn in range(members):
            result = put(result, arrived[turn], (my_line % members - turn) % members)
        return result.reshape((rows,) + blocks.shape[2:])

    def from_sequence(values):
        blocks = values.reshape((members, block_length) + values.shape[1:])
        arrived = []
        for turn in range(members):
            sent = pick(blocks, (my_line % members - turn) % members)
            back = [(target, source) for source, target in there_pairs(turn)]
            arrived.append(lax.ppermute(sent, LINE, back))
        result = jnp.stack(arrived)
        for turn in range(members):
            result = put(result, arrived[turn], (member_of_rank + turn) % members)
        return result

    slot_ids = rank * block_length + jnp.arange(block_length, dtype=jnp.int32)
    valid = slot_ids[None, :] < lengths[:, None]
    spread = jnp.broadcast_to(lengths[:, None], positions.shape)
    digits = jnp.stack(
        [positions // DIGIT, positions % DIGIT, spread // DIGIT, spread % DIGIT], axis=-1
    ).astype(BF)
    digits = jnp.pad(digits, ((0, 0), (0, 0), (0, EXTRA - 4)))
    ff_block = FF // (depth * plane * CHUNKS)
    gateup_rows = gateup_master.shape[0]
    chunk_width = 2 * depth * ff_block
    gateup_blocks = (
        gateup_master.astype(BF)
        .reshape(gateup_rows, 2, depth, plane, CHUNKS, ff_block)
        .transpose(3, 0, 4, 1, 2, 5)
        .reshape(plane, gateup_rows, CHUNKS * chunk_width)
    )
    hidden_wide = jnp.concatenate([hidden, digits], axis=2)
    gateup_blocks = toward(gateup_blocks, PLANE)
    stages = halving_stages(plane)
    for bit in stages[:-1]:
        gateup_blocks = halve(gateup_blocks, PLANE, bit)
    qkv_line, gateup_blocks, hidden_wide = tie(qkv_line, gateup_blocks, hidden_wide)
    qkv_ext = lax.all_gather(qkv_line, PLANE, axis=0)
    moved = to_sequence(hidden_wide)
    gateup_blocks = halve(gateup_blocks, PLANE, stages[-1])
    gateup_mine = in_place(gateup_blocks, PLANE).reshape(plane * gateup_rows, -1)
    masked = jnp.where(valid[..., None], cotangent, jnp.zeros((), BF))
    out_low = out_master.astype(BF)
    moved, gateup_mine, masked, out_low = tie(moved, gateup_mine, masked, out_low)
    out_back_low = to_sequence(masked)
    out_line = depth_gather(out_low)
    down_low = down_master.astype(BF)
    parts = [
        (
            gateup_mine[:, n * chunk_width : (n + 1) * chunk_width],
            down_low[n * ff_block : (n + 1) * ff_block],
        )
        for n in range(CHUNKS)
    ]
    rings = [[pack_weights(*part)] for part in parts]
    turns = [(n, step) for n in range(CHUNKS) for step in range(1, depth)]
    at_once = -(-(depth - 1) // 3)

    def turn_on(count):
        done = []
        for n, _ in turns[: count * at_once]:
            rings[n].append(ring_turn(rings[n][-1]))
            if n not in done:
                done.append(n)
        del turns[: count * at_once]
        return done

    def settle(done, *values):
        flat = []
        for n in done:
            flat += list(rings[n][-1])
        got = tie(*flat, *values)
        for place, n in enumerate(done):
            rings[n][-1] = (got[2 * place], got[2 * place + 1])
        return got[2 * len(done) :]

    first_state = tie(*rings[0][0], out_back_low, out_line)
    rings[0][0] = first_state[:2]
    out_back_low, out_line = first_state[2:]

    numbers = moved[:, width:][:, :4].astype(jnp.int32)
    my_positions = numbers[:, 0] * DIGIT + numbers[:, 1]
    my_length = (numbers[0, 2] * DIGIT + numbers[0, 3]).reshape(1)
    flat_inputs = moved[:, :width].astype(F32)
    all_width = query_width + 2 * key_width
    gains = qkv_ext[..., all_width : all_width + 2].transpose(1, 0, 2, 3).reshape(width, 2)
    gains = gains.astype(F32).T
    first_low = normalize(flat_inputs, gains[0]).astype(BF)
    out_w = lax.all_gather(out_line, PLANE, axis=0)
    cosine, sine = rotary_tables(my_positions)
    member_heads = project(first_low, qkv_ext, cosine, sine, team)
    half = rows // 2
    relay = chips == 4

    def fan_out(value):
        masks = (1, 2) if relay else range(1, chips)
        return {mask: swap(value, "p", mask) for mask in masks}

    def pass_on(first, second):
        low, high = slice(0, half), slice(half, rows)
        return [
            swap(jnp.stack([first[1][low], second[1][low]]), "p", 2),
            swap(jnp.stack([first[2][high], second[2][high]]), "p", 1),
        ]

    dy = fan_out(out_back_low)
    dy_cross = {0: swap(out_back_low, "c", 1)}
    keys = sorted(dy)
    (member_heads,) = settle(turn_on(1), member_heads)
    heads = exchange(member_heads, TEAM).reshape(length_total, -1)
    attended_heads, log_total = attend(my_length, heads, query_each, key_each)
    (attended_heads,) = settle(turn_on(1), attended_heads)
    attended_parts = exchange(attended_heads.reshape(team, rows, -1), TEAM)
    attended_low = jnp.concatenate([attended_parts[u] for u in range(team)], axis=1)
    middle = flat_inputs + gathered_product(attended_low, out_w, width)
    second_low = normalize(middle, gains[1]).astype(BF)
    got = settle(turn_on(1), second_low, dy_cross[0], *[dy[m] for m in keys])
    second_low, dy_cross[0] = got[:2]
    dy = dict(zip(keys, got[2:]))

    weights = {0: unpack_weights(rings[0], *parts[0])}
    cs = fan_out(second_low)
    cs_cross = {0: swap(second_low, "c", 1)}
    kept = {}
    partials = {}

    def run(chunk, block, tokens):
        got = feed(chunk, block, chips, *weights[chunk], tokens, partials.get(block), kept)
        if chunk < CHUNKS - 1:
            partials[block] = (got["o_part"], got["n_part"])
        return got

    results = {}
    results[0] = run(0, 0, (second_low, cs_cross[0], out_back_low, dy_cross[0]))
    names = [(name, 0) for name in ("mixed", "dr", "c_all", "d_all")]
    got = settle(turn_on(1), *[kept[n] for n in names], *[cs[m] for m in keys])
    kept.update(zip(names, got[:4]))
    cs = dict(zip(keys, got[4:]))
    crossed = {mask: swap(jnp.stack([cs[mask], dy[mask]]), "c", 1) for mask in keys}
    halves = pass_on(cs, dy) if relay else []
    for mask in keys:
        results[mask] = run(0, mask, (cs[mask], crossed[mask], dy[mask], crossed[mask]))
    got = settle(turn_on(1), *[kept[n] for n in names], *halves)
    kept.update(zip(names, got[:4]))
    if relay:
        across = jnp.concatenate(got[4:], axis=1)
        crossed[3] = swap(across, "c", 1)
        results[3] = run(0, 3, (across, crossed[3], across, crossed[3]))

    def weight_terms(chunk):
        down_term = jnp.einsum(
            "rc,rk->ck", kept["mixed", chunk], kept["d_all", 0], preferred_element_type=F32
        ).astype(BF)
        gateup_term = jnp.einsum(
            "rc,rk->ck", kept["c_all", 0], kept["dr", chunk], preferred_element_type=F32
        ).astype(BF)
        return down_term, gateup_term

    def packed(terms):
        down_chunks = terms[0].reshape(depth, ff_block, width)
        gateup_chunks = terms[1].reshape(depth, plane * gateup_rows, chunk_width)
        pieces = [
            down_chunks[:, :, at : at + chunk_width] for at in range(0, width, chunk_width)
        ]
        return jnp.concatenate([gateup_chunks] + pieces, axis=1)

    def owners(packed_terms):
        return lax.psum_scatter(packed_terms, DEPTH, scatter_dimension=0)

    terms = weight_terms(0)
    got = settle(turn_on(len(turns)), packed(terms), kept["c_all", 0], kept["d_all", 0])
    kept["c_all", 0], kept["d_all", 0] = got[1:]
    sums = {0: owners(got[0])}
    for chunk in range(1, CHUNKS):
        weights[chunk] = unpack_weights(rings[chunk], *parts[chunk])

    def chip_sum(own, other):
        return (own.astype(F32) + swap(other, "c", 1).astype(F32)).astype(BF)

    norm_sums = {}
    block_order = (3, 1, 2, 0) if relay else (*range(1, chips), 0)
    for chunk in range(1, CHUNKS):
        waiting = None
        for mask in block_order:
            results[mask] = run(chunk, mask, None)
            if chunk < CHUNKS - 1:
                continue
            arriving = swap(results[mask]["n_oth"], "c", 1)
            if waiting is not None:
                before, arrived = waiting
                kept["dr", chunk], arrived = tie(kept["dr", chunk], arrived)
                norm_sums[before] = total_of([results[before]["n_own"], arrived]).astype(BF)
                norm_sums[before] = swap(norm_sums[before], "p", before)
            waiting = mask, arriving
        if chunk == CHUNKS - 1:
            norm_sums[0] = total_of([results[0]["n_own"], waiting[1]]).astype(BF)
    last = CHUNKS - 1
    kept["dr", last], sums[0] = tie(kept["dr", last], sums[0])
    terms = weight_terms(last)
    branch_own = [results[mask]["o_own"] for mask in range(chips)]
    branch_oth = [results[mask]["o_oth"] for mask in range(chips)]
    last_terms, *got = tie(
        packed(terms),
        *[norm_sums[mask] for mask in range(chips)],
        *branch_own,
        *branch_oth,
    )
    norm_back = total_of(got[:chips])
    sums[last] = owners(last_terms)
    branch_own, branch_oth = got[chips : 2 * chips], got[2 * chips :]
    branch = [chip_sum(branch_own[0], branch_oth[0])]
    for mask in range(1, chips):
        branch.append(swap(chip_sum(branch_own[mask], branch_oth[mask]), "p", mask))

    _, second_pull = jax.vjp(normalize, middle, gains[1])
    middle_norm_back, second_gain_grad = second_pull(norm_back)
    middle_back = out_back_low.astype(F32) + middle_norm_back
    branch_low = middle_back.astype(BF)

    attended_back = gathered_back(branch_low, out_w, BF)
    group_width = query_each * HEAD_DIM
    back_blocks = jnp.stack(
        [attended_back[:, u * group_width : (u + 1) * group_width] for u in range(team)]
    )
    back_rows = exchange(back_blocks, TEAM).reshape(length_total, group_width)
    head_grads = attend_back(my_length, heads, back_rows, log_total, query_each, key_each)
    query_back, key_back, value_back = [
        exchange(grad.reshape(team, rows, -1), TEAM) for grad in head_grads
    ]
    projected_back = unturn(query_back, key_back, value_back, cosine, sine)
    first_back = gathered_back(projected_back, qkv_ext, F32)
    _, first_pull = jax.vjp(normalize, flat_inputs, gains[0])
    input_norm_back, first_gain_grad = first_pull(first_back)
    input_back = from_sequence((middle_back + input_norm_back).astype(BF))

    gain_terms = jnp.stack([first_gain_grad, second_gain_grad]).astype(BF).T
    gain_terms = in_ring_order(jnp.pad(gain_terms, ((0, 0), (0, EXTRA - 2))).T, order)
    attention_terms = gradient_terms(
        in_ring_order(first_low, order),
        projected_back,
        in_ring_order(attended_low, order),
        branch_low,
        gain_terms,
    )
    attention_terms, sums[last], *branch = tie(attention_terms, sums[last], *branch)
    attention_sum = scatter_sum(attention_terms, order)
    output = from_sequence((middle + total_of(branch)).astype(BF))

    grown = plane * gateup_rows
    gateup_sum = jnp.concatenate([sums[n][:grown] for n in range(CHUNKS)], axis=1)
    down_grad = jnp.concatenate(
        [
            jnp.concatenate(
                [
                    sums[n][at : at + ff_block].astype(F32)
                    for at in range(grown, sums[n].shape[0], ff_block)
                ],
                axis=1,
            )
            for n in range(CHUNKS)
        ],
        axis=0,
    )
    gateup_sum = toward(gateup_sum.reshape(plane, gateup_rows, CHUNKS * chunk_width), PLANE)
    for bit in stages:
        gateup_sum = halve(gateup_sum, PLANE, bit)
    gateup_grad = (
        in_place(gateup_sum, PLANE)
        .reshape(plane, gateup_rows, CHUNKS, 2, depth, ff_block)
        .transpose(1, 3, 4, 0, 2, 5)
        .reshape(gateup_rows, 2 * FF)
    )
    qkv_grad = attention_sum[:, :all_width].astype(F32)
    out_grad = attention_sum[:, all_width : all_width + width].astype(F32)
    gains_grad = attention_sum[:, all_width + width :][:, :2].astype(F32).T

    qkv_set = adamw_update(
        query_key_value_master,
        query_key_value_first,
        query_key_value_second,
        qkv_grad,
        MODEL_DIM ** (-0.5),
    )
    out_set = adamw_update(out_master, out_first, out_second, out_grad, OUT_RATE)
    gateup_set = adamw_update(
        gateup_master,
        gateup_first,
        gateup_second,
        gateup_grad.astype(F32),
        MODEL_DIM ** (-0.5),
    )
    down_set = adamw_update(
        down_master, down_first, down_second, down_grad, FF ** (-0.5)
    )
    gains_set = adamw_update(gains_master, gains_first, gains_second, gains_grad, GAIN_RATE)
    return (
        (output, input_back) + qkv_set + out_set + gateup_set + down_set + gains_set
    )


def solution(mesh):
    ctx, fsdp = mesh.shape["ctx"], mesh.shape["fsdp"]
    line_count = 4
    fine = Mesh(mesh.devices.reshape(line_count, ctx // line_count, fsdp // 2, 2), EVERY)
    tokens = P(PLANE, DEPTH, None)
    weight = P(EVERY, None)
    gain = P(None, EVERY)
    return jax.shard_map(
        shards,
        mesh=fine,
        in_specs=(tokens, tokens, P(PLANE), P(PLANE, DEPTH)) + (weight,) * 12 + (gain,) * 3,
        out_specs=(tokens, tokens) + (weight,) * 16 + (gain,) * 4,
        check_vma=False,
    )
```
